512 devices in a mesh: row: 16 (over z), col: 32 (over y, x, core).
Axes of the slice: x: 4, y: 4, z: 16, core: 2. Of those that a mesh axis runs over, the one named last changes fastest.
Arguments:
- matrix: float32 [4, 16, 256, 2, 32, 256], P(None, 'row', None, None, 'col'), may hold values from -6 to 6
- panel_t: float32 [256, 4, 16, 256], P('col', None, 'row'), may hold values from -3 to 3
Outputs:
- updated: float32 [4, 16, 256, 2, 32, 256], P(None, 'row', None, None, 'col')
- vectors: float32 [256, 4, 16, 256], P('col', None, 'row')
- band_block: float32 [256, 256], replicated
- reflector_factor: float32 [256, 256], replicated
The draws below stay inside these ranges and needn't reach their ends.
All inputs are finite; a program needn't handle non-finite values.
Results may differ from the reference program's by a relative error of at most 0.00017.
Values sent between devices are 32-bit elements; how exact they have to be, the bound alone decides.
No kernel may reach another device: no remote copies, remote signals or barrier semaphores. Data moves between devices by JAX's collectives and lax.ppermute only.
A program may use at most 64 MiB of HBM per device.

```python
import jax
import jax.numpy as jnp
from jax import lax

NB = 256
TC = 2
TR = 4
N = 16384
N_ROW = 16
N_COL = 32


def draw_panel_t(key, part):
    key = jax.random.fold_in(key, 7)
    base_key, scale_key = jax.random.split(key)
    entries = jnp.clip(jax.random.normal(base_key, (NB, N), jnp.float32), -4.0, 4.0)
    spread = 4.0
    row_scale = jnp.exp(jax.random.uniform(scale_key, (N,), jnp.float32) * jnp.log(spread))
    columns = jnp.arange(N)
    upper_rows = columns < NB
    diagonal = (columns[None, :] == jnp.arange(NB)[:, None]).astype(jnp.float32)
    lower_part = entries * row_scale[None, :] / jnp.sqrt(jnp.float32(N))
    top_part = 2.0 * diagonal + entries / jnp.sqrt(jnp.float32(NB))
    result_panel = jnp.where(upper_rows[None, :], top_part, lower_part)
    return result_panel.reshape(NB, TR, N_ROW, NB)


def block_scale(key, extent, shards, low, high):
    def one(position, shards_of):
        steps = jax.random.uniform(jax.random.fold_in(jax.random.fold_in(key, 6), position), (shards_of,), jnp.float32, low / len(shards), high / len(shards))
        return jnp.repeat(jnp.exp(steps), extent[position] // shards_of).reshape((-1,) + (1,) * (len(extent) - position - 1))

    gain = one(*shards[0])
    for cut in shards[1:]:
        gain = gain * one(*cut)
    return gain


def normal_values(key, shape, scale, most, cuts=(), kind=jnp.bfloat16):
    values = scale * jax.random.normal(key, shape, jnp.float32)
    if cuts:
        values = values * block_scale(key, shape, cuts, -0.22, 0.18)
    return jnp.clip(values, -most, most).astype(kind)


def setup_inputs(seed: int = 0) -> dict:
    splits = jax.random.split(jax.random.key(seed), 3)
    matrix = normal_values(splits[0], (TR, N_ROW, NB, TC, N_COL, NB), 1.0, 6.0, ((1, 16), (4, 32)), jnp.float32)
    panel_t = draw_panel_t(jax.random.fold_in(splits[2], 71), 0)
    return dict(matrix=matrix, panel_t=panel_t)


def matmul(multiplier, multiplicand):
    return jnp.dot(multiplier, multiplicand, precision=lax.Precision.HIGHEST)

def contract_first(multiplier, multiplicand):
    return lax.dot_general(multiplier, multiplicand, (((0,), (0,)), ((), ())), precision=lax.Precision.HIGHEST)

def contract_last(multiplier, multiplicand):
    return lax.dot_general(multiplier, multiplicand, (((1,), (1,)), ((), ())), precision=lax.Precision.HIGHEST)

def lower_solve(factor, right_side, transposed):
    return lax.linalg.triangular_solve(factor, right_side, left_side=True, lower=True, transpose_a=transposed)

def reference(matrix, panel_t):
    dense_matrix = matrix.reshape(N, N)
    panel_cols = panel_t.reshape(NB, N)
    first_factor = jnp.linalg.cholesky(matmul(panel_cols, panel_cols.T))
    orthonormal = lower_solve(first_factor, panel_cols, False)
    band_block = -first_factor.T
    identity = jnp.eye(NB, dtype=jnp.float32)
    vectors_t = jnp.concatenate([orthonormal[:, :NB] + identity, orthonormal[:, NB:]], axis=1)
    top_block = vectors_t[:, :NB]
    top_factor = jnp.linalg.cholesky(contract_first(top_block, top_block))
    reflector = lower_solve(top_factor, lower_solve(top_factor, top_block.T, False), True)
    lower_part = jnp.tril(dense_matrix)
    strict = jnp.tril(dense_matrix, -1)
    products_t = contract_last(vectors_t, lower_part) + matmul(vectors_t, strict)
    curvature = contract_last(vectors_t, products_t)
    mixed_term = matmul(matmul(reflector.T, curvature), reflector)
    update_t = matmul(reflector.T, products_t) - 0.5 * matmul(mixed_term.T, vectors_t)
    correction = contract_first(vectors_t, update_t) + contract_first(update_t, vectors_t)
    updated = jnp.tril(dense_matrix - correction).reshape(matrix.shape)
    return (updated, vectors_t.reshape(panel_t.shape), band_block, reflector)
```

```python
import jax
import jax.numpy as jnp
from jax import lax
from jax.experimental import pallas as pl
from jax.experimental.pallas import tpu as pltpu
from jax.sharding import PartitionSpec as P

NB = 256
TR = 4
TC = 2
N_ROW = 16
N_COL = 32
LANES = 128
BS = 16
SHARE = NB // N_COL
CHUNK = NB // N_ROW
F32 = jnp.float32
VMEM = pl.BlockSpec(memory_space=pltpu.VMEM)
SMEM = pl.BlockSpec(memory_space=pltpu.SMEM)


def call(kernel, outs, scratch=(), n_scalars=0, n_in=1, name=None, flops=0, moved=0):
    return pl.pallas_call(
        kernel,
        out_shape=[jax.ShapeDtypeStruct(shape, F32) for shape in outs],
        in_specs=[SMEM] * n_scalars + [VMEM] * n_in,
        out_specs=[VMEM] * len(outs),
        scratch_shapes=[pltpu.VMEM(shape, F32) for shape in scratch],
        compiler_params=pltpu.CompilerParams(vmem_limit_bytes=40 * 2**20),
        cost_estimate=pl.CostEstimate(flops=flops, bytes_accessed=moved, transcendentals=0),
        name=name,
    )


def exact(a, b, ca=1, cb=0):
    return lax.dot_general(
        a,
        b,
        (((ca,), (cb,)), ((), ())),
        precision=lax.Precision.HIGHEST,
        preferred_element_type=F32,
    )


def split(a):
    high = a.astype(jnp.bfloat16)
    return high, (a - high.astype(F32)).astype(jnp.bfloat16)


def product(a, b, ca=1, cb=0):
    def one(x, y):
        return lax.dot_general(x, y, (((ca,), (cb,)), ((), ())), preferred_element_type=F32)

    return one(a[0], b[0]) + (one(a[0], b[1]) + one(a[1], b[0]))


def linear_tile(ref, tile, tiles):
    halves = NB // LANES
    stride = tiles * halves
    return jnp.concatenate(
        [ref[pl.ds(tile * halves + half, NB, stride), :] for half in range(halves)], axis=1
    )


def matrix_rows(t, u, half):
    return pl.ds((t * NB) * TC * 2 + u * 2 + half, NB, TC * 2)


def matrix_tile(ref, t, u):
    return jnp.concatenate([ref[matrix_rows(t, u, half), :] for half in range(2)], axis=1)


def gram_kernel(place, own_ref, panel_ref, out_ref):
    total = jnp.zeros((SHARE, NB), F32)
    for piece in range(TR * 2):
        total += exact(
            own_ref[pl.ds(piece, SHARE, TR * 2), :], panel_ref[pl.ds(piece, NB, TR * 2), :], 1, 1
        )
    out_ref[:, :NB] = total
    top = jnp.concatenate([own_ref[pl.ds(half, SHARE, TR * 2), :] for half in range(2)], axis=1)
    out_ref[:, NB:] = jnp.where(place[0] == 0, top, 0.0)


def factor_kernel(g_ref, band_ref, linv_ref, refl_ref, a_ref, u_ref):
    n = NB
    steps = n // BS
    rows = lax.broadcasted_iota(jnp.int32, (BS, LANES), 0)
    lanes = lax.broadcasted_iota(jnp.int32, (BS, LANES), 1)
    eye = (rows == lanes).astype(F32)
    wide = lax.broadcasted_iota(jnp.int32, (BS, n), 1)
    full_row = lax.broadcasted_iota(jnp.int32, (n, n), 0)
    full_col = lax.broadcasted_iota(jnp.int32, (n, n), 1)
    a_ref[...] = g_ref[:, :n]

    def advance(base, update, row):
        a_ref[: n - BS, :] = pltpu.roll(base[BS:] - update[BS:], n - BS, 1)
        a_ref[n - BS :, :] = pltpu.roll(row, n - BS, 1)

    def chol_step(step, carry):
        left = n - BS * step
        a = a_ref[...]
        first, second = a[:BS, :LANES], a[:BS, LANES:]
        heads = [jnp.broadcast_to(first[:, k : k + 1], (BS, LANES)) for k in range(BS)]
        inner = eye
        pivots = jnp.ones((BS, LANES), F32)
        for j in range(BS):
            pivot = heads[j][j : j + 1]
            factor = jnp.where(rows > j, heads[j], 0.0) * (1.0 / pivot)
            pivots = jnp.where(rows == j, pivot, pivots)
            for k in range(j + 1, BS):
                heads[k] = heads[k] - factor * heads[k][j : j + 1]
            first = first - factor * first[j : j + 1]
            second = second - factor * second[j : j + 1]
            inner = inner - factor * inner[j : j + 1]
        scale = lax.rsqrt(pivots)
        scale = scale * (1.5 - 0.5 * pivots * scale * scale)
        first, second, inner = first * scale, second * scale, inner * scale
        upper = jnp.concatenate([jnp.where(lanes >= rows, first, 0.0), second], axis=1)
        upper = jnp.where(wide < left, upper, 0.0)
        u_ref[pl.ds(pl.multiple_of(step * BS, BS), BS), :] = pltpu.roll(upper, step * BS, 1)
        row = jnp.concatenate([jnp.where(lanes < BS, inner, first), second], axis=1)
        update = exact(jnp.where(wide >= BS, upper, 0.0), row, 0, 0)
        advance(jnp.where((full_col < BS) & (full_row < left), 0.0, a), update, row)
        return carry

    lax.fori_loop(0, steps, chol_step, 0)
    linv = jnp.where(full_col <= full_row, a_ref[...], 0.0)
    linv_ref[...] = linv
    band_ref[...] = -u_ref[...]
    a_ref[...] = exact(linv, g_ref[:, n:]) + (full_row == full_col).astype(F32)

    def inverse_step(step, carry):
        a = a_ref[...]
        first, second = a[:BS, :LANES], a[:BS, LANES:]
        heads = [jnp.broadcast_to(first[:, k : k + 1], (BS, LANES)) for k in range(BS)]
        first = jnp.where(lanes < BS, eye, first)
        for j in range(BS):
            head = heads[j]
            inverse = 1.0 / head[j : j + 1]

            def put(value):
                scaled = value[j : j + 1] * inverse
                return jnp.where(rows == j, scaled, value - head * scaled)

            for k in range(j + 1, BS):
                heads[k] = put(heads[k])
            first, second = put(first), put(second)
        row = jnp.concatenate([first, second], axis=1)
        update = exact(a[:, :BS], row)
        advance(jnp.where(full_col < BS, 0.0, a), update, row)
        return carry

    lax.fori_loop(0, steps, inverse_step, 0)
    refl_ref[...] = a_ref[...]


def eye_tile():
    return (
        lax.broadcasted_iota(jnp.int32, (NB, NB), 0) == lax.broadcasted_iota(jnp.int32, (NB, NB), 1)
    ).astype(F32)


def symmetric_kernel(
    place, linv_ref, panel_rows_ref, panel_cols_ref, matrix_ref,
    rows_ref, cols_ref, row_terms_ref, mirror_ref, vectors_ref,
):
    row, col = place[0], place[1]
    linv = split(linv_ref[...])
    cols, rows = [], []
    for u in range(TC):
        value = product(linv, split(linear_tile(panel_cols_ref, u, TC)))
        if u == 0:
            value = value + jnp.where(col == 0, eye_tile(), 0.0)
        cols_ref[:, pl.ds(u * NB, NB)] = value
        cols.append(split(value))
    for t in range(TR):
        value = product(linv, split(linear_tile(panel_rows_ref, t, TR)))
        if t == 0:
            value = value + jnp.where(row == 0, eye_tile(), 0.0)
        rows_ref[:, pl.ds(t * NB, NB)] = value
        rows.append(split(value))
    mine = rows_ref[pl.ds(pl.multiple_of(col * SHARE, SHARE), SHARE), :]
    for piece in range(TR * 2):
        vectors_ref[pl.ds(piece, SHARE, TR * 2), :] = mine[:, piece * LANES : (piece + 1) * LANES]

    row_terms_ref[...] = jnp.zeros((NB, TR * NB), F32)
    mirror_ref[...] = jnp.zeros((NB, TC * NB), F32)
    for t in range(TR):
        here = pl.ds(t * NB, NB)
        for u in range(TC):
            there = pl.ds(u * NB, NB)
            i, j = t * N_ROW + row, u * N_COL + col

            @pl.when(i > j)
            def _():
                tile = split(matrix_tile(matrix_ref, t, u))
                row_terms_ref[:, here] += product(cols[u], tile, 1, 1)
                mirror_ref[:, there] += product(rows[t], tile)

            @pl.when(i == j)
            def _():
                tile = matrix_tile(matrix_ref, t, u)
                r = lax.broadcasted_iota(jnp.int32, (NB, NB), 0)
                c = lax.broadcasted_iota(jnp.int32, (NB, NB), 1)
                row_terms_ref[:, here] += product(cols[u], split(jnp.where(r >= c, tile, 0.0)), 1, 1)
                mirror_ref[:, there] += product(rows[t], split(jnp.where(r > c, tile, 0.0)))


def curvature_kernel(share_ref, rows_ref, out_ref):
    out_ref[...] = product(split(share_ref[...]), split(rows_ref[...]), 1, 1)


def update_kernel(
    place, matrix_ref, rows_ref, cols_ref, sums_ref, part_ref, curv_ref, refl_ref, out_ref
):
    row, col = place[0], place[1]
    refl = split(refl_ref[...])
    half_mixed = split(0.5 * product(split(product(refl, split(curv_ref[...]), 0, 0)), refl))
    sides = []
    for u in range(TC):
        span = 2 * CHUNK + SHARE
        summed = jnp.concatenate(
            [part_ref[pl.ds(k * span + u * CHUNK, CHUNK), :] for k in range(N_ROW)], axis=0
        )
        vectors = split(cols_ref[:, pl.ds(u * NB, NB)])
        update = product(refl, split(summed), 0, 0) - product(half_mixed, vectors, 0, 0)
        sides.append((vectors, split(update)))
    for t in range(TR):
        here = pl.ds(t * NB, NB)
        vectors = split(rows_ref[:, here])
        update = split(
            product(refl, split(sums_ref[:, here]), 0, 0) - product(half_mixed, vectors, 0, 0)
        )
        for u in range(TC):
            i, j = t * N_ROW + row, u * N_COL + col

            @pl.when(i >= j)
            def _():
                change = product(vectors, sides[u][1], 0, 0) + product(update, sides[u][0], 0, 0)
                value = matrix_tile(matrix_ref, t, u) - change
                r = lax.broadcasted_iota(jnp.int32, (NB, NB), 0)
                c = lax.broadcasted_iota(jnp.int32, (NB, NB), 1)
                value = jnp.where((r >= c) | (i > j), value, 0.0)
                for half in range(2):
                    out_ref[matrix_rows(t, u, half), :] = value[:, half * LANES : (half + 1) * LANES]

            @pl.when(i < j)
            def _():
                for half in range(2):
                    out_ref[matrix_rows(t, u, half), :] = jnp.zeros((NB, LANES), F32)


def spread(value, axis, count):
    return lax.all_to_all(jnp.tile(value, (count, 1)), axis, 0, 0, tiled=True)


def routes():
    one, two = [], []
    for r in range(N_ROW):
        for c in range(N_COL):
            near = (c // 2) * N_COL + r
            far = near + N_ROW
            one.append((r * N_COL + c, far if c % 2 else near))
            two.append((r * N_COL + c, near if c % 2 else far))
    return one, two


def to_cols(even, odd, col_index):
    one, two = routes()
    flip, low = col_index % 2 == 1, col_index < N_ROW
    first = lax.ppermute(jnp.where(flip, odd, even), ("row", "col"), one)
    second = lax.ppermute(jnp.where(flip, even, odd), ("row", "col"), two)
    return jnp.where(low, first, second), jnp.where(low, second, first)


def to_rows(early, late, col_index):
    one, two = ([(there, here) for here, there in route] for route in routes())
    flip, low = col_index % 2 == 1, col_index < N_ROW
    first = lax.ppermute(jnp.where(low, early, late), ("row", "col"), one)
    second = lax.ppermute(jnp.where(low, late, early), ("row", "col"), two)
    return jnp.where(flip, second, first), jnp.where(flip, first, second)


def body(matrix, panel_t):
    row_index = lax.axis_index("row")
    col_index = lax.axis_index("col")
    place = jnp.stack([row_index, col_index]).astype(jnp.int32)
    stored = matrix.reshape(TR * NB * TC * 2, LANES)
    own = panel_t.reshape(SHARE * TR * 2, LANES)

    with jax.named_scope("panel_rows"):
        panel_rows = spread(own, "col", N_COL)
    with jax.named_scope("panel_cols"):
        by_tile = own.reshape(SHARE, TR, 2, LANES)
        chunk = to_cols(
            by_tile[:, 0::2].reshape(-1, LANES), by_tile[:, 1::2].reshape(-1, LANES), col_index
        )
        panel_cols = spread(jnp.concatenate(chunk, axis=0), "row", N_ROW)
    with jax.named_scope("gram"):
        (partial,) = call(
            gram_kernel, [(SHARE, 2 * NB)], n_scalars=1, n_in=2, name="gram", moved=1 << 20
        )(place, own, panel_rows)
        summed = spread(partial, "row", N_ROW).reshape(N_ROW, SHARE, 2 * NB).sum(0)
        gram = spread(summed, "col", N_COL)
    with jax.named_scope("factor"):
        band, linv, reflector = call(
            factor_kernel,
            [(NB, NB)] * 3,
            scratch=[(NB, NB)] * 2,
            n_in=1,
            name="factor",
            flops=10**10,
            moved=80 << 20,
        )(gram)
    with jax.named_scope("symmetric"):
        rows, cols, row_terms, mirror, vectors = call(
            symmetric_kernel,
            [
                (NB, TR * NB),
                (NB, TC * NB),
                (NB, TR * NB),
                (NB, TC * NB),
                (SHARE * TR * 2, LANES),
            ],
            n_scalars=1,
            n_in=4,
            name="symmetric",
            moved=8 << 20,
        )(place, linv, panel_rows, panel_cols, stored)
    with jax.named_scope("sums"):
        from_cols = (
            lax.all_to_all(mirror, "row", 0, 0, tiled=True).reshape(N_ROW, CHUNK, TC * NB).sum(0)
        )
        from_rows = (
            lax.all_to_all(row_terms, "col", 0, 0, tiled=True).reshape(N_COL, SHARE, TR * NB).sum(0)
        )
        even, odd = to_rows(from_cols[:SHARE], from_cols[SHARE:], col_index)
        tiles = from_rows.reshape(SHARE, TR, NB)
        early, late = to_cols(
            jnp.concatenate([tiles[:, 0], tiles[:, 2]], axis=1),
            jnp.concatenate([tiles[:, 1], tiles[:, 3]], axis=1),
            col_index,
        )
        share = from_rows + jnp.concatenate(
            [even[:, :NB], odd[:, :NB], even[:, NB:], odd[:, NB:]], axis=1
        )
        sums = spread(share, "col", N_COL)
    with jax.named_scope("curvature"):
        (curv,) = call(curvature_kernel, [(SHARE, NB)], n_in=2, name="curvature", moved=1 << 20)(
            share, rows
        )
    with jax.named_scope("sums_cols"):
        chunk = from_cols + jnp.concatenate([early, late], axis=0)
        payload = jnp.concatenate([chunk[:, :NB], chunk[:, NB:], curv], axis=0)
        parts = spread(payload, "row", N_ROW)
    with jax.named_scope("curvature_all"):
        span = 2 * CHUNK + SHARE
        curv = parts.reshape(N_ROW, span, NB)[:, 2 * CHUNK :].sum(0)
        curvature = spread(curv, "col", N_COL)
    with jax.named_scope("update"):
        (updated,) = call(
            update_kernel,
            [(TR * NB * TC * 2, LANES)],
            n_scalars=1,
            n_in=7,
            name="update",
            moved=8 << 20,
        )(place, stored, rows, cols, sums, parts, curvature, reflector)
    return (updated.reshape(matrix.shape), vectors.reshape(panel_t.shape), band, reflector)


def solution(mesh):
    placed = (P(None, "row", None, None, "col", None), P("col", None, "row", None))
    return jax.shard_map(
        body,
        mesh=mesh,
        in_specs=placed,
        out_specs=(P(None, "row", None, None, "col", None), P("col", None, "row", None), P(), P()),
        check_vma=False,
    )
```

```python
import jax
import jax.numpy as jnp
from jax import lax
from jax.experimental import pallas as pl
from jax.experimental.pallas import tpu as pltpu
from jax.sharding import PartitionSpec as P

NB = 256
TR = 4
TC = 2
N_ROW = 16
N_COL = 32
LANES = 128
BS = 16
SHARE = NB // N_COL
CHUNK = NB // N_ROW
F32 = jnp.float32
VMEM = pl.BlockSpec(memory_space=pltpu.VMEM)
SMEM = pl.BlockSpec(memory_space=pltpu.SMEM)


def call(kernel, outs, scratch=(), n_scalars=0, n_in=1, name=None, flops=0, moved=0):
    return pl.pallas_call(
        kernel,
        out_shape=[jax.ShapeDtypeStruct(shape, F32) for shape in outs],
        in_specs=[SMEM] * n_scalars + [VMEM] * n_in,
        out_specs=[VMEM] * len(outs),
        scratch_shapes=[pltpu.VMEM(shape, F32) for shape in scratch],
        compiler_params=pltpu.CompilerParams(vmem_limit_bytes=60 * 2**20),
        cost_estimate=pl.CostEstimate(flops=flops, bytes_accessed=moved, transcendentals=0),
        name=name,
    )


def exact(a, b, ca=1, cb=0):
    return lax.dot_general(
        a,
        b,
        (((ca,), (cb,)), ((), ())),
        precision=lax.Precision.HIGHEST,
        preferred_element_type=F32,
    )


def split(a):
    high = a.astype(jnp.bfloat16)
    return high, (a - high.astype(F32)).astype(jnp.bfloat16)


def product(a, b, ca=1, cb=0):
    def one(x, y):
        return lax.dot_general(x, y, (((ca,), (cb,)), ((), ())), preferred_element_type=F32)

    return one(a[0], b[0]) + (one(a[0], b[1]) + one(a[1], b[0]))


def linear_tile(ref, t):
    return jnp.concatenate([ref[pl.ds(t * 2 + half, NB, TR * 2), :] for half in range(2)], axis=1)


SPAN = CHUNK * TC * 2 + 4 * SHARE


def gathered_tile(ref, u):
    return jnp.concatenate(
        [
            jnp.concatenate(
                [ref[pl.ds(k * SPAN + u * 2 + half, CHUNK, TC * 2), :] for k in range(N_ROW)], axis=0
            )
            for half in range(2)
        ],
        axis=1,
    )


def matrix_rows(t, u, half):
    return pl.ds((t * NB) * TC * 2 + u * 2 + half, NB, TC * 2)


def matrix_tile(ref, t, u):
    return jnp.concatenate([ref[matrix_rows(t, u, half), :] for half in range(2)], axis=1)


def gram_kernel(place, own_ref, panel_ref, early_ref, late_ref, out_ref):
    total = jnp.zeros((SHARE, NB), F32)
    for piece in range(TR * 2):
        total += exact(
            own_ref[pl.ds(piece, SHARE, TR * 2), :], panel_ref[pl.ds(piece, NB, TR * 2), :], 1, 1
        )
    half_chunk = SHARE * TC * 2
    out_ref[:half_chunk, :] = early_ref[...]
    out_ref[half_chunk : 2 * half_chunk, :] = late_ref[...]
    for half in range(2):
        at = 2 * half_chunk + half * SHARE
        out_ref[pl.ds(at, SHARE), :] = total[:, half * LANES : (half + 1) * LANES]
        top = own_ref[pl.ds(half, SHARE, TR * 2), :]
        out_ref[pl.ds(at + 2 * SHARE, SHARE), :] = jnp.where(place[0] == 0, top, 0.0)


def gathered_columns(g_ref, quarters):
    return jnp.concatenate(
        [
            jnp.concatenate(
                [g_ref[pl.ds((4 * k + q) * SHARE, SHARE), :] for k in range(N_COL)], axis=0
            )
            for q in quarters
        ],
        axis=1,
    )


def factor_kernel(g_ref, band_ref, linv_ref, refl_ref, a_ref, u_ref):
    n = NB
    steps = n // BS
    rows = lax.broadcasted_iota(jnp.int32, (BS, LANES), 0)
    lanes = lax.broadcasted_iota(jnp.int32, (BS, LANES), 1)
    eye = (rows == lanes).astype(F32)
    wide = lax.broadcasted_iota(jnp.int32, (BS, n), 1)
    full_row = lax.broadcasted_iota(jnp.int32, (n, n), 0)
    full_col = lax.broadcasted_iota(jnp.int32, (n, n), 1)
    a_ref[...] = gathered_columns(g_ref, (0, 1))

    def advance(base, update, row):
        a_ref[: n - BS, :] = pltpu.roll(base[BS:] - update[BS:], n - BS, 1)
        a_ref[n - BS :, :] = pltpu.roll(row, n - BS, 1)

    def chol_step(step, carry):
        left = n - BS * step
        a = a_ref[...]
        first, second = a[:BS, :LANES], a[:BS, LANES:]
        heads = [jnp.broadcast_to(first[:, k : k + 1], (BS, LANES)) for k in range(BS)]
        inner = eye
        pivots = jnp.ones((BS, LANES), F32)
        for j in range(BS):
            pivot = heads[j][j : j + 1]
            factor = jnp.where(rows > j, heads[j], 0.0) * (1.0 / pivot)
            pivots = jnp.where(rows == j, pivot, pivots)
            for k in range(j + 1, BS):
                heads[k] = heads[k] - factor * heads[k][j : j + 1]
            first = first - factor * first[j : j + 1]
            second = second - factor * second[j : j + 1]
            inner = inner - factor * inner[j : j + 1]
        scale = lax.rsqrt(pivots)
        scale = scale * (1.5 - 0.5 * pivots * scale * scale)
        first, second, inner = first * scale, second * scale, inner * scale
        upper = jnp.concatenate([jnp.where(lanes >= rows, first, 0.0), second], axis=1)
        upper = jnp.where(wide < left, upper, 0.0)
        u_ref[pl.ds(pl.multiple_of(step * BS, BS), BS), :] = pltpu.roll(upper, step * BS, 1)
        row = jnp.concatenate([jnp.where(lanes < BS, inner, first), second], axis=1)
        update = exact(jnp.where(wide >= BS, upper, 0.0), row, 0, 0)
        advance(jnp.where((full_col < BS) & (full_row < left), 0.0, a), update, row)
        return carry

    lax.fori_loop(0, steps, chol_step, 0)
    linv = jnp.where(full_col <= full_row, a_ref[...], 0.0)
    linv_ref[...] = linv
    band_ref[...] = -u_ref[...]
    a_ref[...] = exact(linv, gathered_columns(g_ref, (2, 3))) + (full_row == full_col).astype(F32)

    def inverse_step(step, carry):
        a = a_ref[...]
        first, second = a[:BS, :LANES], a[:BS, LANES:]
        heads = [jnp.broadcast_to(first[:, k : k + 1], (BS, LANES)) for k in range(BS)]
        first = jnp.where(lanes < BS, eye, first)
        for j in range(BS):
            head = heads[j]
            inverse = 1.0 / head[j : j + 1]

            def put(value):
                scaled = value[j : j + 1] * inverse
                return jnp.where(rows == j, scaled, value - head * scaled)

            for k in range(j + 1, BS):
                heads[k] = put(heads[k])
            first, second = put(first), put(second)
        row = jnp.concatenate([first, second], axis=1)
        update = exact(a[:, :BS], row)
        advance(jnp.where(full_col < BS, 0.0, a), update, row)
        return carry

    lax.fori_loop(0, steps, inverse_step, 0)
    refl_ref[...] = a_ref[...]


def tile_place(place, t, u):
    return t * N_ROW + place[0], u * N_COL + place[1]


def ordering():
    r = lax.broadcasted_iota(jnp.int32, (NB, NB), 0)
    c = lax.broadcasted_iota(jnp.int32, (NB, NB), 1)
    return r, c


def mirror_kernel(place, panel_ref, matrix_ref, out_ref):
    out_ref[...] = jnp.zeros((NB, TC * NB), F32)
    for t in range(TR):
        rows = split(linear_tile(panel_ref, t))
        for u in range(TC):
            here = pl.ds(u * NB, NB)
            i, j = tile_place(place, t, u)

            @pl.when(i > j)
            def _():
                out_ref[:, here] += product(rows, split(matrix_tile(matrix_ref, t, u)))

            @pl.when(i == j)
            def _():
                r, c = ordering()
                tile = jnp.where(r > c, matrix_tile(matrix_ref, t, u), 0.0)
                out_ref[:, here] += product(rows, split(tile))


def symmetric_kernel(place, band_ref, panel_ref, matrix_ref, out_ref):
    factor = -jnp.transpose(band_ref[...])
    out_ref[...] = jnp.zeros((NB, TR * NB), F32)
    cols = []
    for u in range(TC):
        value = gathered_tile(panel_ref, u)
        if u == 0:
            value = value + jnp.where(place[1] == 0, factor, 0.0)
        cols.append(split(value))
    for t in range(TR):
        here = pl.ds(t * NB, NB)
        for u in range(TC):
            i, j = tile_place(place, t, u)

            @pl.when(i > j)
            def _():
                out_ref[:, here] += product(cols[u], split(matrix_tile(matrix_ref, t, u)), 1, 1)

            @pl.when(i == j)
            def _():
                r, c = ordering()
                tile = jnp.where(r >= c, matrix_tile(matrix_ref, t, u), 0.0)
                out_ref[:, here] += product(cols[u], split(tile), 1, 1)

        if t == 0:

            @pl.when((place[0] == 0) & (place[1] == 0))
            def _():
                r, c = ordering()
                tile = jnp.where(r > c, matrix_tile(matrix_ref, 0, 0), 0.0)
                out_ref[:, here] += product(split(factor), split(tile))


def vectors_kernel(
    place, linv_ref, refl_ref, panel_rows_ref, panel_cols_ref,
    rows_ref, cols_ref, both_ref, vectors_ref,
):
    linv = split(linv_ref[...])
    r, c = ordering()
    eye = (r == c).astype(F32)
    both_ref[...] = product(split(refl_ref[...]), linv, 0, 0)
    for u in range(TC):
        value = product(linv, split(gathered_tile(panel_cols_ref, u)))
        if u == 0:
            value = value + jnp.where(place[1] == 0, eye, 0.0)
        cols_ref[:, pl.ds(u * NB, NB)] = value
    for t in range(TR):
        value = product(linv, split(linear_tile(panel_rows_ref, t)))
        if t == 0:
            value = value + jnp.where(place[0] == 0, eye, 0.0)
        rows_ref[:, pl.ds(t * NB, NB)] = value
    mine = rows_ref[pl.ds(pl.multiple_of(place[1] * SHARE, SHARE), SHARE), :]
    for piece in range(TR * 2):
        vectors_ref[pl.ds(piece, SHARE, TR * 2), :] = mine[:, piece * LANES : (piece + 1) * LANES]


PART = (TR + 1) * SHARE
DEAL = (TC + 1 + TR) * SHARE


def share_kernel(recv_ref, even_ref, odd_ref, rows_ref, out_ref):
    total = recv_ref[pl.ds(0, SHARE), :]
    for k in range(1, N_COL):
        total = total + recv_ref[pl.ds(k * SHARE, SHARE), :]
    mirrored = [even_ref[:, :NB], odd_ref[:, :NB], even_ref[:, NB:], odd_ref[:, NB:]]
    total = total + jnp.concatenate(mirrored, axis=1)
    for t in range(TR):
        out_ref[pl.ds(t * SHARE, SHARE), :] = total[:, t * NB : (t + 1) * NB]
    out_ref[pl.ds(TR * SHARE, SHARE), :] = product(split(total), split(rows_ref[...]), 1, 1)


def deal_kernel(own_ref, part_ref, out_ref):
    curved = part_ref[pl.ds(TR * SHARE, SHARE), :]
    for r in range(1, N_ROW):
        curved = curved + part_ref[pl.ds(r * PART + TR * SHARE, SHARE), :]
    own = own_ref[: TR * SHARE, :]
    for c in range(N_COL):
        for u in range(TC):
            t = u * (N_COL // N_ROW) + c // N_ROW
            out_ref[pl.ds(c * DEAL + u * SHARE, SHARE), :] = part_ref[
                pl.ds((c % N_ROW) * PART + t * SHARE, SHARE), :
            ]
        out_ref[pl.ds(c * DEAL + TC * SHARE, SHARE), :] = curved
        out_ref[pl.ds(c * DEAL + (TC + 1) * SHARE, TR * SHARE), :] = own


def dealt(ref, slot):
    return jnp.concatenate(
        [ref[pl.ds(c * DEAL + slot * SHARE, SHARE), :] for c in range(N_COL)], axis=0
    )


def update_kernel(
    place, matrix_ref, rows_ref, cols_ref, dealt_ref, refl_ref, both_ref, out_ref
):
    both = split(both_ref[...])
    curved = split(product(both, split(dealt(dealt_ref, TC))))
    half_mixed = split(0.5 * product(curved, split(refl_ref[...])))
    sides = []
    for u in range(TC):
        vectors = split(cols_ref[:, pl.ds(u * NB, NB)])
        update = product(both, split(dealt(dealt_ref, u))) - product(half_mixed, vectors)
        sides.append((vectors, split(update)))
    for t in range(TR):
        here = pl.ds(t * NB, NB)
        vectors = split(rows_ref[:, here])
        update = split(product(both, split(dealt(dealt_ref, TC + 1 + t))) - product(half_mixed, vectors))
        for u in range(TC):
            i, j = tile_place(place, t, u)

            @pl.when(i >= j)
            def _():
                change = product(vectors, sides[u][1], 0, 0) + product(update, sides[u][0], 0, 0)
                value = matrix_tile(matrix_ref, t, u) - change
                r, c = ordering()
                value = jnp.where((r >= c) | (i > j), value, 0.0)
                for half in range(2):
                    out_ref[matrix_rows(t, u, half), :] = value[:, half * LANES : (half + 1) * LANES]

            @pl.when(i < j)
            def _():
                for half in range(2):
                    out_ref[matrix_rows(t, u, half), :] = jnp.zeros((NB, LANES), F32)


def spread(value, axis, count):
    return lax.all_to_all(jnp.tile(value, (count, 1)), axis, 0, 0, tiled=True)


def routes():
    one, two = [], []
    for r in range(N_ROW):
        for c in range(N_COL):
            near = (c // 2) * N_COL + r
            far = near + N_ROW
            one.append((r * N_COL + c, far if c % 2 else near))
            two.append((r * N_COL + c, near if c % 2 else far))
    return one, two


def to_cols(even, odd, col_index):
    one, two = routes()
    flip, low = col_index % 2 == 1, col_index < N_ROW
    first = lax.ppermute(jnp.where(flip, odd, even), ("row", "col"), one)
    second = lax.ppermute(jnp.where(flip, even, odd), ("row", "col"), two)
    return jnp.where(low, first, second), jnp.where(low, second, first)


def to_rows(early, late, col_index):
    one, two = ([(there, here) for here, there in route] for route in routes())
    flip, low = col_index % 2 == 1, col_index < N_ROW
    first = lax.ppermute(jnp.where(low, early, late), ("row", "col"), one)
    second = lax.ppermute(jnp.where(low, late, early), ("row", "col"), two)
    return jnp.where(flip, second, first), jnp.where(flip, first, second)


def body(matrix, panel_t):
    row_index = lax.axis_index("row")
    col_index = lax.axis_index("col")
    place = jnp.stack([row_index, col_index]).astype(jnp.int32)
    stored = matrix.reshape(TR * NB * TC * 2, LANES)
    own = panel_t.reshape(SHARE * TR * 2, LANES)

    with jax.named_scope("panel"):
        by_tile = own.reshape(SHARE, TR, 2, LANES)
        chunk = to_cols(
            by_tile[:, 0::2].reshape(-1, LANES), by_tile[:, 1::2].reshape(-1, LANES), col_index
        )
        panel_rows, chunk = lax.optimization_barrier((spread(own, "col", N_COL), chunk))
    with jax.named_scope("gram"):
        (payload,) = call(
            gram_kernel, [(SPAN, LANES)], n_scalars=1, n_in=4, name="gram", moved=1 << 20
        )(place, own, panel_rows, *chunk)
        panel_cols = lax.all_gather(payload, "row", tiled=True)
        summed = panel_cols.reshape(N_ROW, SPAN, LANES)[:, CHUNK * TC * 2 :].sum(0)
        gram = spread(summed, "col", N_COL)
    with jax.named_scope("mirror"):
        (mirror,) = call(
            mirror_kernel, [(NB, TC * NB)], n_scalars=1, n_in=2, name="mirror", moved=4 << 20
        )(place, panel_rows, stored)
        gram, mirror = lax.optimization_barrier((gram, mirror))
        from_cols = (
            lax.all_to_all(mirror, "row", 0, 0, tiled=True).reshape(N_ROW, CHUNK, TC * NB).sum(0)
        )
    with jax.named_scope("factor"):
        band, linv, reflector = call(
            factor_kernel,
            [(NB, NB)] * 3,
            scratch=[(NB, NB)] * 2,
            n_in=1,
            name="factor",
            flops=10**10,
            moved=80 << 20,
        )(gram)
    with jax.named_scope("symmetric"):
        (row_terms,) = call(
            symmetric_kernel, [(NB, TR * NB)], n_scalars=1, n_in=3, name="symmetric", moved=4 << 20
        )(place, band, panel_cols, stored)
    with jax.named_scope("vectors"):
        rows, cols, both, vectors = call(
            vectors_kernel,
            [(NB, TR * NB), (NB, TC * NB), (NB, NB), (SHARE * TR * 2, LANES)],
            n_scalars=1,
            n_in=4,
            name="vectors",
            moved=4 << 20,
        )(place, linv, reflector, panel_rows, panel_cols)
    with jax.named_scope("sums"):
        received = lax.all_to_all(row_terms, "col", 0, 0, tiled=True)
        even, odd = to_rows(from_cols[:SHARE], from_cols[SHARE:], col_index)
        (payload,) = call(share_kernel, [(PART, NB)], n_in=4, name="share", moved=2 << 20)(
            received, even, odd, rows
        )
        parts = lax.all_gather(payload, "row", tiled=True)
    with jax.named_scope("deal"):
        (deal,) = call(deal_kernel, [(N_COL * DEAL, NB)], n_in=2, name="deal", moved=3 << 20)(
            payload, parts
        )
        deal = lax.all_to_all(deal, "col", 0, 0, tiled=True)
    with jax.named_scope("update"):
        (updated,) = call(
            update_kernel,
            [(TR * NB * TC * 2, LANES)],
            n_scalars=1,
            n_in=6,
            name="update",
            moved=8 << 20,
        )(place, stored, rows, cols, deal, reflector, both)
    return (updated.reshape(matrix.shape), vectors.reshape(panel_t.shape), band, reflector)


def solution(mesh):
    placed = (P(None, "row", None, None, "col", None), P("col", None, "row", None))
    return jax.shard_map(
        body,
        mesh=mesh,
        in_specs=placed,
        out_specs=(P(None, "row", None, None, "col", None), P("col", None, "row", None), P(), P()),
        check_vma=False,
    )
```

```python
import jax
import jax.numpy as jnp
from jax import lax
from jax.experimental import pallas as pl
from jax.experimental.pallas import tpu as pltpu
from jax.sharding import PartitionSpec as P

NB = 256
TR = 4
TC = 2
N_ROW = 16
N_COL = 32
LANES = 128
BS = 16
SHARE = NB // N_COL
CHUNK = NB // N_ROW
F32 = jnp.float32
VMEM = pl.BlockSpec(memory_space=pltpu.VMEM)
SMEM = pl.BlockSpec(memory_space=pltpu.SMEM)


ANY = pl.BlockSpec(memory_space=pl.ANY)


def call(
    kernel, outs, scratch=(), n_scalars=0, n_in=1, n_any=0, any_out=False, copies=0,
    name=None, flops=0, moved=0,
):
    buffers = [pltpu.VMEM(shape, F32) for shape in scratch]
    if copies:
        buffers.append(pltpu.SemaphoreType.DMA((copies,)))
    return pl.pallas_call(
        kernel,
        out_shape=[jax.ShapeDtypeStruct(shape, F32) for shape in outs],
        in_specs=[SMEM] * n_scalars + [VMEM] * n_in + [ANY] * n_any,
        out_specs=[ANY if any_out else VMEM] * len(outs),
        scratch_shapes=buffers,
        compiler_params=pltpu.CompilerParams(vmem_limit_bytes=40 * 2**20),
        cost_estimate=pl.CostEstimate(flops=flops, bytes_accessed=moved, transcendentals=0),
        name=name,
    )


def exact(a, b, ca=1, cb=0):
    return lax.dot_general(
        a,
        b,
        (((ca,), (cb,)), ((), ())),
        precision=lax.Precision.HIGHEST,
        preferred_element_type=F32,
    )


def split(a):
    high = a.astype(jnp.bfloat16)
    return high, (a - high.astype(F32)).astype(jnp.bfloat16)


def product(a, b, ca=1, cb=0):
    def one(x, y):
        return lax.dot_general(x, y, (((ca,), (cb,)), ((), ())), preferred_element_type=F32)

    return one(a[0], b[0]) + (one(a[0], b[1]) + one(a[1], b[0]))


def linear_tile(ref, t):
    return jnp.concatenate([ref[pl.ds(t * 2 + half, NB, TR * 2), :] for half in range(2)], axis=1)


SPAN = CHUNK * TC * 2 + 4 * SHARE


def gathered_tile(ref, u):
    return jnp.concatenate(
        [
            jnp.concatenate(
                [ref[pl.ds(k * SPAN + u * 2 + half, CHUNK, TC * 2), :] for k in range(N_ROW)], axis=0
            )
            for half in range(2)
        ],
        axis=1,
    )


def matrix_rows(t, u, half):
    return pl.ds((t * NB) * TC * 2 + u * 2 + half, NB, TC * 2)


def matrix_tile(ref, t, u):
    return jnp.concatenate([ref[matrix_rows(t, u, half), :] for half in range(2)], axis=1)


def gram_kernel(place, own_ref, early_ref, late_ref, panel_ref, out_ref):
    total = jnp.zeros((SHARE, NB), F32)
    for piece in range(TR * 2):
        total += exact(
            own_ref[pl.ds(piece, SHARE, TR * 2), :], panel_ref[pl.ds(piece, NB, TR * 2), :], 1, 1
        )
    half_chunk = SHARE * TC * 2
    out_ref[:half_chunk, :] = early_ref[...]
    out_ref[half_chunk : 2 * half_chunk, :] = late_ref[...]
    for half in range(2):
        at = 2 * half_chunk + half * SHARE
        out_ref[pl.ds(at, SHARE), :] = total[:, half * LANES : (half + 1) * LANES]
        top = own_ref[pl.ds(half, SHARE, TR * 2), :]
        out_ref[pl.ds(at + 2 * SHARE, SHARE), :] = jnp.where(place[0] == 0, top, 0.0)


def gathered_columns(g_ref, quarters):
    return jnp.concatenate(
        [
            jnp.concatenate(
                [g_ref[pl.ds((4 * k + q) * SHARE, SHARE), :] for k in range(N_COL)], axis=0
            )
            for q in quarters
        ],
        axis=1,
    )


def stacked(a, b):
    def three(x):
        high = x.astype(jnp.bfloat16)
        x = x - high.astype(F32)
        mid = x.astype(jnp.bfloat16)
        return high, mid, (x - mid.astype(F32)).astype(jnp.bfloat16)

    a1, a2, a3 = three(a)
    b1, b2, b3 = three(b)
    return lax.dot_general(
        jnp.concatenate([a1, a1, a1, a2, a2, a3], axis=0),
        jnp.concatenate([b1, b2, b3, b1, b2, b1], axis=0),
        (((0,), (0,)), ((), ())),
        preferred_element_type=F32,
    )


def block_iotas():
    rows = lax.broadcasted_iota(jnp.int32, (BS, LANES), 0)
    lanes = lax.broadcasted_iota(jnp.int32, (BS, LANES), 1)
    wide = lax.broadcasted_iota(jnp.int32, (BS, NB), 1)
    return rows, lanes, wide


def turn(a_ref, base, row):
    a_ref[: NB - BS, :] = pltpu.roll(base[BS:], NB - BS, 1)
    a_ref[NB - BS :, :] = pltpu.roll(row, NB - BS, 1)


def unturned(value, a_ref, row_ref):
    turned = pltpu.roll(value, BS, 1)
    a_ref[:BS, :] = turned[NB - BS :]
    a_ref[BS:, :] = turned[: NB - BS]
    row_ref[...] = turned[NB - BS :]


def lane_spread(first):
    return [jnp.broadcast_to(first[:, k : k + 1], (BS, LANES)) for k in range(BS)]


def cholesky(g_ref, band_ref, linv_ref, a_ref, u_ref, row_ref, multiplier_ref):
    rows, lanes, wide = block_iotas()
    full_row, full_col = ordering()
    unturned(gathered_columns(g_ref, (0, 1)), a_ref, row_ref)
    multiplier_ref[...] = jnp.zeros((BS, NB), F32)

    def step_of(step, carry):
        left = NB - BS * step
        begun = step > 0
        a, last, multiplier = a_ref[...], row_ref[...], multiplier_ref[...]
        top = jnp.where((wide < BS) & begun, 0.0, a[BS : 2 * BS])
        top = pltpu.roll(top - stacked(multiplier[:, BS : 2 * BS], last), NB - BS, 1)
        first, second = top[:, :LANES], top[:, LANES:]
        heads = lane_spread(first)
        inner = (rows == lanes).astype(F32)
        pivots = jnp.ones((BS, LANES), F32)
        for j in range(BS):
            pivot = heads[j][j : j + 1]
            factor = jnp.where(rows > j, heads[j], 0.0) * (1.0 / pivot)
            pivots = jnp.where(rows == j, pivot, pivots)
            for k in range(j + 1, BS):
                heads[k] = heads[k] - factor * heads[k][j : j + 1]
            first = first - factor * first[j : j + 1]
            second = second - factor * second[j : j + 1]
            inner = inner - factor * inner[j : j + 1]
        scale = lax.rsqrt(pivots)
        scale = scale * (1.5 - 0.5 * pivots * scale * scale)
        first, second, inner = first * scale, second * scale, inner * scale
        upper = jnp.concatenate([jnp.where(lanes >= rows, first, 0.0), second], axis=1)
        upper = jnp.where(wide < left, upper, 0.0)
        u_ref[pl.ds(pl.multiple_of(step * BS, BS), BS), :] = pltpu.roll(upper, step * BS, 1)
        row_ref[...] = jnp.concatenate([jnp.where(lanes < BS, inner, first), second], axis=1)
        multiplier_ref[...] = jnp.where(wide >= BS, upper, 0.0)
        kept = jnp.where((full_col < BS) & (full_row < left + BS) & begun, 0.0, a)
        turn(a_ref, kept - stacked(multiplier, last), last)
        return carry

    lax.fori_loop(0, NB // BS, step_of, 0)
    turn(a_ref, a_ref[...], row_ref[...])
    linv_ref[...] = jnp.where(full_col <= full_row, a_ref[...], 0.0)
    band_ref[...] = -u_ref[...]


def reflector_factor(g_ref, linv_ref, refl_ref, a_ref, row_ref):
    rows, lanes, _ = block_iotas()
    full_row, full_col = ordering()
    top_block = exact(linv_ref[...], gathered_columns(g_ref, (2, 3)))
    unturned(top_block + (full_row == full_col).astype(F32), a_ref, row_ref)

    def step_of(step, carry):
        begun = step > 0
        a, last = a_ref[...], row_ref[...]
        kept = jnp.where((full_col < BS) & begun, 0.0, a)
        column = jnp.where(begun, a[:, :BS], 0.0)
        top = pltpu.roll(kept[BS : 2 * BS] - exact(column[BS : 2 * BS], last), NB - BS, 1)
        first, second = top[:, :LANES], top[:, LANES:]
        heads = lane_spread(first)
        first = jnp.where(lanes < BS, (rows == lanes).astype(F32), first)
        for j in range(BS):
            head = heads[j]
            inverse = 1.0 / head[j : j + 1]

            def put(value):
                scaled = value[j : j + 1] * inverse
                return jnp.where(rows == j, scaled, value - head * scaled)

            for k in range(j + 1, BS):
                heads[k] = put(heads[k])
            first, second = put(first), put(second)
        row_ref[...] = jnp.concatenate([first, second], axis=1)
        turn(a_ref, kept - exact(column, last), last)
        return carry

    lax.fori_loop(0, NB // BS, step_of, 0)
    a, last = a_ref[...], row_ref[...]
    turn(a_ref, jnp.where(full_col < BS, 0.0, a) - exact(a[:, :BS], last), last)
    refl_ref[...] = a_ref[...]


def factor_kernel(g_ref, band_ref, linv_ref, refl_ref, a_ref, u_ref, row_ref, multiplier_ref):
    cholesky(g_ref, band_ref, linv_ref, a_ref, u_ref, row_ref, multiplier_ref)
    reflector_factor(g_ref, linv_ref, refl_ref, a_ref, row_ref)


def tile_place(place, t, u):
    return t * N_ROW + place[0], u * N_COL + place[1]


def ordering():
    r = lax.broadcasted_iota(jnp.int32, (NB, NB), 0)
    c = lax.broadcasted_iota(jnp.int32, (NB, NB), 1)
    return r, c


def mirror_kernel(place, panel_ref, matrix_ref, out_ref):
    out_ref[...] = jnp.zeros((NB, TC * NB), F32)
    for t in range(TR):
        rows = split(linear_tile(panel_ref, t))
        for u in range(TC):
            here = pl.ds(u * NB, NB)
            i, j = tile_place(place, t, u)

            @pl.when(i > j)
            def _():
                out_ref[:, here] += product(rows, split(matrix_tile(matrix_ref, t, u)))

            @pl.when(i == j)
            def _():
                r, c = ordering()
                tile = jnp.where(r > c, matrix_tile(matrix_ref, t, u), 0.0)
                out_ref[:, here] += product(rows, split(tile))


def row_copies(matrix_hbm, matrix_ref, sems, first):
    rows = matrix_ref.shape[0] // TR
    return [
        pltpu.make_async_copy(
            matrix_hbm.at[pl.ds(t * rows, rows)], matrix_ref.at[pl.ds(t * rows, rows)],
            sems.at[first + t],
        )
        for t in range(TR)
    ]


def symmetric_kernel(
    place, band_ref, matrix_ref, panel_hbm, out_hbm, panel_ref, out_ref, sems
):
    panel_copy = pltpu.make_async_copy(panel_hbm, panel_ref, sems.at[0])
    panel_copy.start()
    out_copies = []
    factor = -jnp.transpose(band_ref[...])
    out_ref[...] = jnp.zeros((NB, TR * NB), F32)
    panel_copy.wait()
    cols = []
    for u in range(TC):
        value = gathered_tile(panel_ref, u)
        if u == 0:
            value = value + jnp.where(place[1] == 0, factor, 0.0)
        cols.append(split(value))
    for t in range(TR):
        here = pl.ds(t * NB, NB)
        for u in range(TC):
            i, j = tile_place(place, t, u)

            @pl.when(i > j)
            def _():
                out_ref[:, here] += product(cols[u], split(matrix_tile(matrix_ref, t, u)), 1, 1)

            @pl.when(i == j)
            def _():
                r, c = ordering()
                tile = jnp.where(r >= c, matrix_tile(matrix_ref, t, u), 0.0)
                out_ref[:, here] += product(cols[u], split(tile), 1, 1)

        if t == 0:

            @pl.when((place[0] == 0) & (place[1] == 0))
            def _():
                r, c = ordering()
                tile = jnp.where(r > c, matrix_tile(matrix_ref, 0, 0), 0.0)
                out_ref[:, here] += product(split(factor), split(tile))

        out_copies.append(
            pltpu.make_async_copy(out_ref.at[:, here], out_hbm.at[:, here], sems.at[1 + t])
        )
        out_copies[t].start()
    for copy in out_copies:
        copy.wait()


def vectors_kernel(
    place, linv_ref, refl_ref, panel_rows_ref, panel_cols_ref,
    rows_ref, cols_ref, both_ref, vectors_ref,
):
    linv = split(linv_ref[...])
    r, c = ordering()
    eye = (r == c).astype(F32)
    both_ref[...] = product(split(refl_ref[...]), linv, 0, 0)
    for u in range(TC):
        value = product(linv, split(gathered_tile(panel_cols_ref, u)))
        if u == 0:
            value = value + jnp.where(place[1] == 0, eye, 0.0)
        cols_ref[:, pl.ds(u * NB, NB)] = value
    for t in range(TR):
        value = product(linv, split(linear_tile(panel_rows_ref, t)))
        if t == 0:
            value = value + jnp.where(place[0] == 0, eye, 0.0)
        rows_ref[:, pl.ds(t * NB, NB)] = value
    mine = rows_ref[pl.ds(pl.multiple_of(place[1] * SHARE, SHARE), SHARE), :]
    for piece in range(TR * 2):
        vectors_ref[pl.ds(piece, SHARE, TR * 2), :] = mine[:, piece * LANES : (piece + 1) * LANES]


PART = (TR + 1) * SHARE
DEAL = (TC + 1 + TR) * SHARE


def share_kernel(recv_ref, even_ref, odd_ref, rows_ref, out_ref):
    total = recv_ref[pl.ds(0, SHARE), :]
    for k in range(1, N_COL):
        total = total + recv_ref[pl.ds(k * SHARE, SHARE), :]
    mirrored = [even_ref[:, :NB], odd_ref[:, :NB], even_ref[:, NB:], odd_ref[:, NB:]]
    total = total + jnp.concatenate(mirrored, axis=1)
    for t in range(TR):
        out_ref[pl.ds(t * SHARE, SHARE), :] = total[:, t * NB : (t + 1) * NB]
    out_ref[pl.ds(TR * SHARE, SHARE), :] = product(split(total), split(rows_ref[...]), 1, 1)


def deal_kernel(own_ref, part_ref, out_hbm, out_ref, sems):
    curved = part_ref[pl.ds(TR * SHARE, SHARE), :]
    for r in range(1, N_ROW):
        curved = curved + part_ref[pl.ds(r * PART + TR * SHARE, SHARE), :]
    own = own_ref[: TR * SHARE, :]
    copies = []
    group = N_COL // 4
    for c in range(N_COL):
        for u in range(TC):
            t = u * (N_COL // N_ROW) + c // N_ROW
            out_ref[pl.ds(c * DEAL + u * SHARE, SHARE), :] = part_ref[
                pl.ds((c % N_ROW) * PART + t * SHARE, SHARE), :
            ]
        out_ref[pl.ds(c * DEAL + TC * SHARE, SHARE), :] = curved
        out_ref[pl.ds(c * DEAL + (TC + 1) * SHARE, TR * SHARE), :] = own
        if c % group == group - 1:
            at = pl.ds((c + 1 - group) * DEAL, group * DEAL)
            copies.append(
                pltpu.make_async_copy(out_ref.at[at], out_hbm.at[at], sems.at[len(copies)])
            )
            copies[-1].start()
    for copy in copies:
        copy.wait()


def dealt(ref, slot):
    return jnp.concatenate(
        [ref[pl.ds(c * DEAL + slot * SHARE, SHARE), :] for c in range(N_COL)], axis=0
    )


def update_kernel(
    place, refl_ref, both_ref, cols_ref, rows_ref, matrix_ref, dealt_hbm, out_hbm,
    dealt_ref, out_ref, sems,
):
    dealt_copy = pltpu.make_async_copy(dealt_hbm, dealt_ref, sems.at[0])
    dealt_copy.start()
    out_copies = row_copies(out_ref, out_hbm, sems, 1)
    both = split(both_ref[...])
    refl = split(refl_ref[...])
    dealt_copy.wait()
    curved = split(product(both, split(dealt(dealt_ref, TC))))
    half_mixed = split(0.5 * product(curved, refl))
    sides = []
    for u in range(TC):
        vectors = split(cols_ref[:, pl.ds(u * NB, NB)])
        update = product(both, split(dealt(dealt_ref, u))) - product(half_mixed, vectors)
        sides.append((vectors, split(update)))
    for t in range(TR):
        here = pl.ds(t * NB, NB)
        vectors = split(rows_ref[:, here])
        update = split(
            product(both, split(dealt(dealt_ref, TC + 1 + t))) - product(half_mixed, vectors)
        )
        for u in range(TC):
            i, j = tile_place(place, t, u)

            @pl.when(i >= j)
            def _():
                change = product(vectors, sides[u][1], 0, 0) + product(update, sides[u][0], 0, 0)
                value = matrix_tile(matrix_ref, t, u) - change
                r, c = ordering()
                value = jnp.where((r >= c) | (i > j), value, 0.0)
                for half in range(2):
                    out_ref[matrix_rows(t, u, half), :] = value[:, half * LANES : (half + 1) * LANES]

            @pl.when(i < j)
            def _():
                for half in range(2):
                    out_ref[matrix_rows(t, u, half), :] = jnp.zeros((NB, LANES), F32)

        out_copies[t].start()
    for copy in out_copies:
        copy.wait()


def spread(value, axis, count):
    return lax.all_to_all(jnp.tile(value, (count, 1)), axis, 0, 0, tiled=True)


def routes():
    one, two = [], []
    for r in range(N_ROW):
        for c in range(N_COL):
            near = (c // 2) * N_COL + r
            far = near + N_ROW
            one.append((r * N_COL + c, far if c % 2 else near))
            two.append((r * N_COL + c, near if c % 2 else far))
    return one, two


def to_cols(even, odd, col_index):
    one, two = routes()
    flip, low = col_index % 2 == 1, col_index < N_ROW
    first = lax.ppermute(jnp.where(flip, odd, even), ("row", "col"), one)
    second = lax.ppermute(jnp.where(flip, even, odd), ("row", "col"), two)
    return jnp.where(low, first, second), jnp.where(low, second, first)


def to_rows(early, late, col_index):
    one, two = ([(there, here) for here, there in route] for route in routes())
    flip, low = col_index % 2 == 1, col_index < N_ROW
    first = lax.ppermute(jnp.where(low, early, late), ("row", "col"), one)
    second = lax.ppermute(jnp.where(low, late, early), ("row", "col"), two)
    return jnp.where(flip, second, first), jnp.where(flip, first, second)


def body(matrix, panel_t):
    row_index = lax.axis_index("row")
    col_index = lax.axis_index("col")
    place = jnp.stack([row_index, col_index]).astype(jnp.int32)
    stored = matrix.reshape(TR * NB * TC * 2, LANES)
    own = panel_t.reshape(SHARE * TR * 2, LANES)

    with jax.named_scope("panel"):
        by_tile = own.reshape(SHARE, TR, 2, LANES)
        chunk = to_cols(
            by_tile[:, 0::2].reshape(-1, LANES), by_tile[:, 1::2].reshape(-1, LANES), col_index
        )
        panel_rows, chunk = lax.optimization_barrier((spread(own, "col", N_COL), chunk))
    with jax.named_scope("gram"):
        (payload,) = call(
            gram_kernel, [(SPAN, LANES)], n_scalars=1, n_in=4, name="gram", moved=1 << 20
        )(place, own, *chunk, panel_rows)
        panel_cols = lax.all_gather(payload, "row", tiled=True)
        summed = panel_cols.reshape(N_ROW, SPAN, LANES)[:, CHUNK * TC * 2 :].sum(0)
        gram = spread(summed, "col", N_COL)
    with jax.named_scope("mirror"):
        (mirror,) = call(
            mirror_kernel, [(NB, TC * NB)], n_scalars=1, n_in=2, name="mirror", moved=4 << 20
        )(place, panel_rows, stored)
        gram, mirror = lax.optimization_barrier((gram, mirror))
        from_cols = (
            lax.all_to_all(mirror, "row", 0, 0, tiled=True).reshape(N_ROW, CHUNK, TC * NB).sum(0)
        )
    with jax.named_scope("factor"):
        band, linv, reflector = call(
            factor_kernel,
            [(NB, NB)] * 3,
            scratch=[(NB, NB)] * 2 + [(BS, NB)] * 2,
            n_in=1,
            name="factor",
            flops=10**10,
            moved=80 << 20,
        )(gram)
    with jax.named_scope("symmetric"):
        (row_terms,) = call(
            symmetric_kernel, [(NB, TR * NB)],
            scratch=[(N_ROW * SPAN, LANES), (NB, TR * NB)],
            n_scalars=1, n_in=2, n_any=1, any_out=True, copies=1 + TR,
            name="symmetric", moved=4 << 20,
        )(place, band, stored, panel_cols)
    with jax.named_scope("vectors"):
        rows, cols, both, vectors = call(
            vectors_kernel,
            [(NB, TR * NB), (NB, TC * NB), (NB, NB), (SHARE * TR * 2, LANES)],
            n_scalars=1,
            n_in=4,
            name="vectors",
            moved=4 << 20,
        )(place, linv, reflector, panel_rows, panel_cols)
    with jax.named_scope("sums"):
        received = lax.all_to_all(row_terms, "col", 0, 0, tiled=True)
        even, odd = to_rows(from_cols[:SHARE], from_cols[SHARE:], col_index)
        (payload,) = call(share_kernel, [(PART, NB)], n_in=4, name="share", moved=2 << 20)(
            received, even, odd, rows
        )
        parts = lax.all_gather(payload, "row", tiled=True)
    with jax.named_scope("deal"):
        (deal,) = call(
            deal_kernel, [(N_COL * DEAL, NB)], scratch=[(N_COL * DEAL, NB)], n_in=2, any_out=True,
            copies=4, name="deal", moved=3 << 20,
        )(payload, parts)
        deal = lax.all_to_all(deal, "col", 0, 0, tiled=True)
    with jax.named_scope("update"):
        (updated,) = call(
            update_kernel,
            [(TR * NB * TC * 2, LANES)],
            scratch=[(N_COL * DEAL, NB), (TR * NB * TC * 2, LANES)],
            n_scalars=1,
            n_in=5,
            n_any=1,
            any_out=True,
            copies=1 + TR,
            name="update",
            moved=8 << 20,
        )(place, reflector, both, cols, rows, stored, deal)
    return (updated.reshape(matrix.shape), vectors.reshape(panel_t.shape), band, reflector)


def solution(mesh):
    placed = (P(None, "row", None, None, "col", None), P("col", None, "row", None))
    return jax.shard_map(
        body,
        mesh=mesh,
        in_specs=placed,
        out_specs=(P(None, "row", None, None, "col", None), P("col", None, "row", None), P(), P()),
        check_vma=False,
    )
```

```python
import jax
import jax.numpy as jnp
from jax import lax
from jax.experimental import pallas as pl
from jax.experimental.pallas import tpu as pltpu
from jax.sharding import PartitionSpec as P

NB = 256
TR = 4
TC = 2
N_ROW = 16
N_COL = 32
LANES = 128
BS = 16
SHARE = NB // N_COL
CHUNK = NB // N_ROW
F32 = jnp.float32
VMEM = pl.BlockSpec(memory_space=pltpu.VMEM)
SMEM = pl.BlockSpec(memory_space=pltpu.SMEM)


ANY = pl.BlockSpec(memory_space=pl.ANY)


def call(
    kernel, outs, scratch=(), n_scalars=0, n_in=1, n_any=0, any_out=False, copies=0,
    name=None, flops=0, moved=0,
):
    buffers = [pltpu.VMEM(shape, F32) for shape in scratch]
    if copies:
        buffers.append(pltpu.SemaphoreType.DMA((copies,)))
    return pl.pallas_call(
        kernel,
        out_shape=[jax.ShapeDtypeStruct(shape, F32) for shape in outs],
        in_specs=[SMEM] * n_scalars + [VMEM] * n_in + [ANY] * n_any,
        out_specs=[ANY if any_out else VMEM] * len(outs),
        scratch_shapes=buffers,
        compiler_params=pltpu.CompilerParams(vmem_limit_bytes=40 * 2**20),
        cost_estimate=pl.CostEstimate(flops=flops, bytes_accessed=moved, transcendentals=0),
        name=name,
    )


def exact(a, b, ca=1, cb=0):
    return lax.dot_general(
        a,
        b,
        (((ca,), (cb,)), ((), ())),
        precision=lax.Precision.HIGHEST,
        preferred_element_type=F32,
    )


def split(a):
    high = a.astype(jnp.bfloat16)
    return high, (a - high.astype(F32)).astype(jnp.bfloat16)


def product(a, b, ca=1, cb=0):
    def one(x, y):
        return lax.dot_general(x, y, (((ca,), (cb,)), ((), ())), preferred_element_type=F32)

    return one(a[0], b[0]) + (one(a[0], b[1]) + one(a[1], b[0]))


def linear_tile(ref, t):
    return jnp.concatenate([ref[pl.ds(t * 2 + half, NB, TR * 2), :] for half in range(2)], axis=1)


SPAN = CHUNK * TC * 2 + 4 * SHARE


def gathered_tile(ref, u):
    return jnp.concatenate(
        [
            jnp.concatenate(
                [ref[pl.ds(k * SPAN + u * 2 + half, CHUNK, TC * 2), :] for k in range(N_ROW)], axis=0
            )
            for half in range(2)
        ],
        axis=1,
    )


def matrix_rows(t, u, half):
    return pl.ds((t * NB) * TC * 2 + u * 2 + half, NB, TC * 2)


def matrix_tile(ref, t, u):
    return jnp.concatenate([ref[matrix_rows(t, u, half), :] for half in range(2)], axis=1)


def gram_kernel(place, own_ref, early_ref, late_ref, panel_ref, out_ref):
    total = jnp.zeros((SHARE, NB), F32)
    for piece in range(TR * 2):
        total += exact(
            own_ref[pl.ds(piece, SHARE, TR * 2), :], panel_ref[pl.ds(piece, NB, TR * 2), :], 1, 1
        )
    half_chunk = SHARE * TC * 2
    out_ref[:half_chunk, :] = early_ref[...]
    out_ref[half_chunk : 2 * half_chunk, :] = late_ref[...]
    for half in range(2):
        at = 2 * half_chunk + half * SHARE
        out_ref[pl.ds(at, SHARE), :] = total[:, half * LANES : (half + 1) * LANES]
        top = own_ref[pl.ds(half, SHARE, TR * 2), :]
        out_ref[pl.ds(at + 2 * SHARE, SHARE), :] = jnp.where(place[0] == 0, top, 0.0)


def gathered_columns(g_ref, quarters):
    return jnp.concatenate(
        [
            jnp.concatenate(
                [g_ref[pl.ds((4 * k + q) * SHARE, SHARE), :] for k in range(N_COL)], axis=0
            )
            for q in quarters
        ],
        axis=1,
    )


def stacked(a, b):
    def three(x):
        high = x.astype(jnp.bfloat16)
        x = x - high.astype(F32)
        mid = x.astype(jnp.bfloat16)
        return high, mid, (x - mid.astype(F32)).astype(jnp.bfloat16)

    a1, a2, a3 = three(a)
    b1, b2, b3 = three(b)
    return lax.dot_general(
        jnp.concatenate([a1, a1, a1, a2, a2, a3], axis=0),
        jnp.concatenate([b1, b2, b3, b1, b2, b1], axis=0),
        (((0,), (0,)), ((), ())),
        preferred_element_type=F32,
    )


def block_iotas():
    rows = lax.broadcasted_iota(jnp.int32, (BS, LANES), 0)
    lanes = lax.broadcasted_iota(jnp.int32, (BS, LANES), 1)
    wide = lax.broadcasted_iota(jnp.int32, (BS, NB), 1)
    return rows, lanes, wide


def turn(a_ref, base, row):
    a_ref[: NB - BS, :] = pltpu.roll(base[BS:], NB - BS, 1)
    a_ref[NB - BS :, :] = pltpu.roll(row, NB - BS, 1)


def unturned(value, a_ref, row_ref):
    turned = pltpu.roll(value, BS, 1)
    a_ref[:BS, :] = turned[NB - BS :]
    a_ref[BS:, :] = turned[: NB - BS]
    row_ref[...] = turned[NB - BS :]


def lane_spread(first):
    return [jnp.broadcast_to(first[:, k : k + 1], (BS, LANES)) for k in range(BS)]


def cholesky(g_ref, band_ref, linv_ref, a_ref, u_ref, row_ref, multiplier_ref):
    rows, lanes, wide = block_iotas()
    full_row, full_col = ordering()
    unturned(gathered_columns(g_ref, (0, 1)), a_ref, row_ref)
    multiplier_ref[...] = jnp.zeros((BS, NB), F32)

    def step_of(step, carry):
        left = NB - BS * step
        begun = step > 0
        a, last, multiplier = a_ref[...], row_ref[...], multiplier_ref[...]
        top = jnp.where((wide < BS) & begun, 0.0, a[BS : 2 * BS])
        top = pltpu.roll(top - stacked(multiplier[:, BS : 2 * BS], last), NB - BS, 1)
        first, second = top[:, :LANES], top[:, LANES:]
        heads = lane_spread(first)
        inner = (rows == lanes).astype(F32)
        pivots = jnp.ones((BS, LANES), F32)
        for j in range(BS):
            pivot = heads[j][j : j + 1]
            factor = jnp.where(rows > j, heads[j], 0.0) * (1.0 / pivot)
            pivots = jnp.where(rows == j, pivot, pivots)
            for k in range(j + 1, BS):
                heads[k] = heads[k] - factor * heads[k][j : j + 1]
            first = first - factor * first[j : j + 1]
            second = second - factor * second[j : j + 1]
            inner = inner - factor * inner[j : j + 1]
        scale = lax.rsqrt(pivots)
        scale = scale * (1.5 - 0.5 * pivots * scale * scale)
        first, second, inner = first * scale, second * scale, inner * scale
        upper = jnp.concatenate([jnp.where(lanes >= rows, first, 0.0), second], axis=1)
        upper = jnp.where(wide < left, upper, 0.0)
        u_ref[pl.ds(pl.multiple_of(step * BS, BS), BS), :] = pltpu.roll(upper, step * BS, 1)
        row_ref[...] = jnp.concatenate([jnp.where(lanes < BS, inner, first), second], axis=1)
        multiplier_ref[...] = jnp.where(wide >= BS, upper, 0.0)
        kept = jnp.where((full_col < BS) & (full_row < left + BS) & begun, 0.0, a)
        turn(a_ref, kept - stacked(multiplier, last), last)
        return carry

    lax.fori_loop(0, NB // BS, step_of, 0)
    turn(a_ref, a_ref[...], row_ref[...])
    linv_ref[...] = jnp.where(full_col <= full_row, a_ref[...], 0.0)
    band_ref[...] = -u_ref[...]


def reflector_factor(g_ref, linv_ref, refl_ref, a_ref, row_ref):
    rows, lanes, _ = block_iotas()
    full_row, full_col = ordering()
    top_block = exact(linv_ref[...], gathered_columns(g_ref, (2, 3)))
    unturned(top_block + (full_row == full_col).astype(F32), a_ref, row_ref)

    def step_of(step, carry):
        begun = step > 0
        a, last = a_ref[...], row_ref[...]
        kept = jnp.where((full_col < BS) & begun, 0.0, a)
        column = jnp.where(begun, a[:, :BS], 0.0)
        top = pltpu.roll(kept[BS : 2 * BS] - exact(column[BS : 2 * BS], last), NB - BS, 1)
        first, second = top[:, :LANES], top[:, LANES:]
        heads = lane_spread(first)
        first = jnp.where(lanes < BS, (rows == lanes).astype(F32), first)
        for j in range(BS):
            head = heads[j]
            inverse = 1.0 / head[j : j + 1]

            def put(value):
                scaled = value[j : j + 1] * inverse
                return jnp.where(rows == j, scaled, value - head * scaled)

            for k in range(j + 1, BS):
                heads[k] = put(heads[k])
            first, second = put(first), put(second)
        row_ref[...] = jnp.concatenate([first, second], axis=1)
        turn(a_ref, kept - exact(column, last), last)
        return carry

    lax.fori_loop(0, NB // BS, step_of, 0)
    a, last = a_ref[...], row_ref[...]
    turn(a_ref, jnp.where(full_col < BS, 0.0, a) - exact(a[:, :BS], last), last)
    refl_ref[...] = a_ref[...]


def reflector_kernel(g_ref, linv_ref, refl_ref, both_ref, a_ref, row_ref):
    reflector_factor(g_ref, linv_ref, refl_ref, a_ref, row_ref)
    both_ref[...] = product(split(refl_ref[...]), split(linv_ref[...]), 0, 0)


def tile_place(place, t, u):
    return t * N_ROW + place[0], u * N_COL + place[1]


def ordering():
    r = lax.broadcasted_iota(jnp.int32, (NB, NB), 0)
    c = lax.broadcasted_iota(jnp.int32, (NB, NB), 1)
    return r, c


def mirror_kernel(place, panel_ref, matrix_ref, keep_ref, send_ref, sum_ref):
    sum_ref[...] = jnp.zeros((NB, TC * NB), F32)
    for t in range(TR):
        rows = split(linear_tile(panel_ref, t))
        for u in range(TC):
            here = pl.ds(u * NB, NB)
            i, j = tile_place(place, t, u)

            @pl.when(i > j)
            def _():
                sum_ref[:, here] += product(rows, split(matrix_tile(matrix_ref, t, u)))

            @pl.when(i == j)
            def _():
                r, c = ordering()
                tile = jnp.where(r > c, matrix_tile(matrix_ref, t, u), 0.0)
                sum_ref[:, here] += product(rows, split(tile))

    for parity in range(2):

        @pl.when(place[0] % 2 == parity)
        def _():
            for k in range(N_ROW // 2):
                at = pl.ds(k * CHUNK, CHUNK)
                keep_ref[at, :] = sum_ref[pl.ds((2 * k + parity) * CHUNK, CHUNK), :]
                send_ref[at, :] = sum_ref[pl.ds((2 * k + 1 - parity) * CHUNK, CHUNK), :]


def row_copies(matrix_hbm, matrix_ref, sems, first):
    rows = matrix_ref.shape[0] // TR
    return [
        pltpu.make_async_copy(
            matrix_hbm.at[pl.ds(t * rows, rows)], matrix_ref.at[pl.ds(t * rows, rows)],
            sems.at[first + t],
        )
        for t in range(TR)
    ]


def symmetric_kernel(
    place, band_ref, matrix_ref, panel_hbm, out_hbm, panel_ref, out_ref, sems
):
    panel_copy = pltpu.make_async_copy(panel_hbm, panel_ref, sems.at[0])
    panel_copy.start()
    out_copies = []
    factor = -jnp.transpose(band_ref[...])
    out_ref[...] = jnp.zeros((NB, TR * NB), F32)
    panel_copy.wait()
    cols = []
    for u in range(TC):
        value = gathered_tile(panel_ref, u)
        if u == 0:
            value = value + jnp.where(place[1] == 0, factor, 0.0)
        cols.append(split(value))
    for t in range(TR):
        here = pl.ds(t * NB, NB)
        for u in range(TC):
            i, j = tile_place(place, t, u)

            @pl.when(i > j)
            def _():
                out_ref[:, here] += product(cols[u], split(matrix_tile(matrix_ref, t, u)), 1, 1)

            @pl.when(i == j)
            def _():
                r, c = ordering()
                tile = jnp.where(r >= c, matrix_tile(matrix_ref, t, u), 0.0)
                out_ref[:, here] += product(cols[u], split(tile), 1, 1)

        if t == 0:

            @pl.when((place[0] == 0) & (place[1] == 0))
            def _():
                r, c = ordering()
                tile = jnp.where(r > c, matrix_tile(matrix_ref, 0, 0), 0.0)
                out_ref[:, here] += product(split(factor), split(tile))

        out_copies.append(
            pltpu.make_async_copy(out_ref.at[:, here], out_hbm.at[:, here], sems.at[1 + t])
        )
        out_copies[t].start()
    for copy in out_copies:
        copy.wait()


def vectors_kernel(
    place, linv_ref, panel_rows_ref, panel_cols_ref, rows_ref, cols_ref, vectors_ref,
):
    linv = split(linv_ref[...])
    r, c = ordering()
    eye = (r == c).astype(F32)
    for u in range(TC):
        value = product(linv, split(gathered_tile(panel_cols_ref, u)))
        if u == 0:
            value = value + jnp.where(place[1] == 0, eye, 0.0)
        cols_ref[:, pl.ds(u * NB, NB)] = value
    for t in range(TR):
        value = product(linv, split(linear_tile(panel_rows_ref, t)))
        if t == 0:
            value = value + jnp.where(place[0] == 0, eye, 0.0)
        rows_ref[:, pl.ds(t * NB, NB)] = value
    mine = rows_ref[pl.ds(pl.multiple_of(place[1] * SHARE, SHARE), SHARE), :]
    for piece in range(TR * 2):
        vectors_ref[pl.ds(piece, SHARE, TR * 2), :] = mine[:, piece * LANES : (piece + 1) * LANES]


PART = (TR + 1) * SHARE
DEAL = (TC + 1 + TR) * SHARE


def share_kernel(even_ref, odd_ref, recv_hbm, rows_hbm, out_ref, recv_ref, rows_ref, sems):
    recv_copy = pltpu.make_async_copy(recv_hbm, recv_ref, sems.at[0])
    rows_copy = pltpu.make_async_copy(rows_hbm, rows_ref, sems.at[1])
    recv_copy.start()
    rows_copy.start()
    recv_copy.wait()
    total = recv_ref[pl.ds(0, SHARE), :]
    for k in range(1, N_COL):
        total = total + recv_ref[pl.ds(k * SHARE, SHARE), :]
    mirrored = [even_ref[:, :NB], odd_ref[:, :NB], even_ref[:, NB:], odd_ref[:, NB:]]
    total = total + jnp.concatenate(mirrored, axis=1)
    for t in range(TR):
        out_ref[pl.ds(t * SHARE, SHARE), :] = total[:, t * NB : (t + 1) * NB]
    rows_copy.wait()
    out_ref[pl.ds(TR * SHARE, SHARE), :] = product(split(total), split(rows_ref[...]), 1, 1)


def deal_kernel(own_ref, part_ref, out_hbm, out_ref, sems):
    curved = part_ref[pl.ds(TR * SHARE, SHARE), :]
    for r in range(1, N_ROW):
        curved = curved + part_ref[pl.ds(r * PART + TR * SHARE, SHARE), :]
    own = own_ref[: TR * SHARE, :]
    copies = []
    group = N_COL // 4
    for c in range(N_COL):
        for u in range(TC):
            t = u * (N_COL // N_ROW) + c // N_ROW
            out_ref[pl.ds(c * DEAL + u * SHARE, SHARE), :] = part_ref[
                pl.ds((c % N_ROW) * PART + t * SHARE, SHARE), :
            ]
        out_ref[pl.ds(c * DEAL + TC * SHARE, SHARE), :] = curved
        out_ref[pl.ds(c * DEAL + (TC + 1) * SHARE, TR * SHARE), :] = own
        if c % group == group - 1:
            at = pl.ds((c + 1 - group) * DEAL, group * DEAL)
            copies.append(
                pltpu.make_async_copy(out_ref.at[at], out_hbm.at[at], sems.at[len(copies)])
            )
            copies[-1].start()
    for copy in copies:
        copy.wait()


def dealt(ref, slot):
    return jnp.concatenate(
        [ref[pl.ds(c * DEAL + slot * SHARE, SHARE), :] for c in range(N_COL)], axis=0
    )


def update_kernel(
    place, matrix_ref, both_hbm, refl_hbm, dealt_hbm, cols_hbm, rows_hbm, out_hbm,
    both_ref, refl_ref, dealt_ref, cols_ref, rows_ref, out_ref, sems,
):
    pairs = (
        (both_hbm, both_ref), (refl_hbm, refl_ref), (dealt_hbm, dealt_ref),
        (cols_hbm, cols_ref), (rows_hbm, rows_ref),
    )
    copies = [
        pltpu.make_async_copy(source, target, sems.at[k])
        for k, (source, target) in enumerate(pairs)
    ]
    for copy in copies:
        copy.start()
    out_copies = row_copies(out_ref, out_hbm, sems, len(copies))
    copies[0].wait()
    both = split(both_ref[...])
    copies[1].wait()
    refl = split(refl_ref[...])
    copies[2].wait()
    curved = split(product(both, split(dealt(dealt_ref, TC))))
    half_mixed = split(0.5 * product(curved, refl))
    copies[3].wait()
    sides = []
    for u in range(TC):
        vectors = split(cols_ref[:, pl.ds(u * NB, NB)])
        update = product(both, split(dealt(dealt_ref, u))) - product(half_mixed, vectors)
        sides.append((vectors, split(update)))
    copies[4].wait()
    for t in range(TR):
        here = pl.ds(t * NB, NB)
        vectors = split(rows_ref[:, here])
        update = split(
            product(both, split(dealt(dealt_ref, TC + 1 + t))) - product(half_mixed, vectors)
        )
        for u in range(TC):
            i, j = tile_place(place, t, u)

            @pl.when(i >= j)
            def _():
                change = product(vectors, sides[u][1], 0, 0) + product(update, sides[u][0], 0, 0)
                value = matrix_tile(matrix_ref, t, u) - change
                r, c = ordering()
                value = jnp.where((r >= c) | (i > j), value, 0.0)
                for half in range(2):
                    out_ref[matrix_rows(t, u, half), :] = value[:, half * LANES : (half + 1) * LANES]

            @pl.when(i < j)
            def _():
                for half in range(2):
                    out_ref[matrix_rows(t, u, half), :] = jnp.zeros((NB, LANES), F32)

        out_copies[t].start()
    for copy in out_copies:
        copy.wait()


def spread(value, axis, count):
    return lax.all_to_all(jnp.tile(value, (count, 1)), axis, 0, 0, tiled=True)


def routes():
    one, two = [], []
    for r in range(N_ROW):
        for c in range(N_COL):
            near = (c // 2) * N_COL + r
            far = near + N_ROW
            one.append((r * N_COL + c, far if c % 2 else near))
            two.append((r * N_COL + c, near if c % 2 else far))
    return one, two


def to_cols(even, odd, col_index):
    one, two = routes()
    flip, low = col_index % 2 == 1, col_index < N_ROW
    first = lax.ppermute(jnp.where(flip, odd, even), ("row", "col"), one)
    second = lax.ppermute(jnp.where(flip, even, odd), ("row", "col"), two)
    return jnp.where(low, first, second), jnp.where(low, second, first)


def to_rows(early, late, col_index):
    one, two = ([(there, here) for here, there in route] for route in routes())
    flip, low = col_index % 2 == 1, col_index < N_ROW
    first = lax.ppermute(jnp.where(low, early, late), ("row", "col"), one)
    second = lax.ppermute(jnp.where(low, late, early), ("row", "col"), two)
    return jnp.where(flip, second, first), jnp.where(flip, first, second)


def body(matrix, panel_t):
    row_index = lax.axis_index("row")
    col_index = lax.axis_index("col")
    place = jnp.stack([row_index, col_index]).astype(jnp.int32)
    stored = matrix.reshape(TR * NB * TC * 2, LANES)
    own = panel_t.reshape(SHARE * TR * 2, LANES)

    with jax.named_scope("panel"):
        by_tile = own.reshape(SHARE, TR, 2, LANES)
        chunk = to_cols(
            by_tile[:, 0::2].reshape(-1, LANES), by_tile[:, 1::2].reshape(-1, LANES), col_index
        )
        panel_rows, chunk = lax.optimization_barrier((spread(own, "col", N_COL), chunk))
    with jax.named_scope("gram"):
        (payload,) = call(
            gram_kernel, [(SPAN, LANES)], n_scalars=1, n_in=4, name="gram", moved=1 << 20
        )(place, own, *chunk, panel_rows)
        panel_cols = lax.all_gather(payload, "row", tiled=True)
        summed = panel_cols.reshape(N_ROW, SPAN, LANES)[:, CHUNK * TC * 2 :].sum(0)
        gram = spread(summed, "col", N_COL)
    with jax.named_scope("mirror"):
        keep, send = call(
            mirror_kernel, [(NB // 2, TC * NB)] * 2, scratch=[(NB, TC * NB)], n_scalars=1, n_in=2,
            name="mirror", moved=4 << 20,
        )(place, panel_rows, stored)
        mirror = keep + lax.ppermute(send, "row", [(r, r ^ 1) for r in range(N_ROW)])
        gram, mirror = lax.optimization_barrier((gram, mirror))
        parities = [list(range(parity, N_ROW, 2)) for parity in range(2)]
        mirror = lax.all_to_all(mirror, "row", 0, 0, axis_index_groups=parities, tiled=True)
        from_cols = mirror.reshape(N_ROW // 2, CHUNK, TC * NB).sum(0)
    with jax.named_scope("factor"):
        band, linv = call(
            cholesky,
            [(NB, NB)] * 2,
            scratch=[(NB, NB)] * 2 + [(BS, NB)] * 2,
            n_in=1,
            name="cholesky",
            flops=5 * 10**9,
            moved=40 << 20,
        )(gram)
    with jax.named_scope("symmetric"):
        (row_terms,) = call(
            symmetric_kernel, [(NB, TR * NB)],
            scratch=[(N_ROW * SPAN, LANES), (NB, TR * NB)],
            n_scalars=1, n_in=2, n_any=1, any_out=True, copies=1 + TR,
            name="symmetric", moved=4 << 20,
        )(place, band, stored, panel_cols)
    with jax.named_scope("vectors"):
        rows, cols, vectors = call(
            vectors_kernel,
            [(NB, TR * NB), (NB, TC * NB), (SHARE * TR * 2, LANES)],
            n_scalars=1,
            n_in=3,
            name="vectors",
            moved=4 << 20,
        )(place, linv, panel_rows, panel_cols)
    with jax.named_scope("sums"):
        received = lax.all_to_all(row_terms, "col", 0, 0, tiled=True)
        even, odd = to_rows(from_cols[:SHARE], from_cols[SHARE:], col_index)
        (payload,) = call(
            share_kernel, [(PART, NB)], scratch=[(NB, TR * NB)] * 2, n_in=2, n_any=2, copies=2,
            name="share", moved=2 << 20,
        )(even, odd, received, rows)
        parts = lax.all_gather(payload, "row", tiled=True)
    with jax.named_scope("deal"):
        (deal,) = call(
            deal_kernel, [(N_COL * DEAL, NB)], scratch=[(N_COL * DEAL, NB)], n_in=2, any_out=True,
            copies=4, name="deal", moved=3 << 20,
        )(payload, parts)
        deal, gram, linv = lax.optimization_barrier((deal, gram, linv))
        deal = lax.all_to_all(deal, "col", 0, 0, tiled=True)
    with jax.named_scope("reflector"):
        reflector, both = call(
            reflector_kernel,
            [(NB, NB)] * 2,
            scratch=[(NB, NB), (BS, NB)],
            n_in=2,
            name="reflector",
            flops=5 * 10**9,
            moved=40 << 20,
        )(gram, linv)
    with jax.named_scope("update"):
        (updated,) = call(
            update_kernel,
            [(TR * NB * TC * 2, LANES)],
            scratch=[
                (NB, NB),
                (NB, NB),
                (N_COL * DEAL, NB),
                (NB, TC * NB),
                (NB, TR * NB),
                (TR * NB * TC * 2, LANES),
            ],
            n_scalars=1,
            n_in=1,
            n_any=5,
            any_out=True,
            copies=5 + TR,
            name="update",
            moved=8 << 20,
        )(place, stored, both, reflector, deal, cols, rows)
    return (updated.reshape(matrix.shape), vectors.reshape(panel_t.shape), band, reflector)


def solution(mesh):
    placed = (P(None, "row", None, None, "col", None), P("col", None, "row", None))
    return jax.shard_map(
        body,
        mesh=mesh,
        in_specs=placed,
        out_specs=(P(None, "row", None, None, "col", None), P("col", None, "row", None), P(), P()),
        check_vma=False,
    )
```

```python
import jax
import jax.numpy as jnp
from jax import lax
from jax.experimental import pallas as pl
from jax.experimental.pallas import tpu as pltpu
from jax.sharding import PartitionSpec as P

NB = 256
TR = 4
TC = 2
N_ROW = 16
N_COL = 32
LANES = 128
BS = 16
SHARE = NB // N_COL
CHUNK = NB // N_ROW
F32 = jnp.float32
VMEM = pl.BlockSpec(memory_space=pltpu.VMEM)
SMEM = pl.BlockSpec(memory_space=pltpu.SMEM)


ANY = pl.BlockSpec(memory_space=pl.ANY)


def call(
    kernel, outs, scratch=(), n_scalars=0, n_in=1, n_any=0, any_out=False, copies=0,
    name=None, flops=0, moved=0, megabytes=40,
):
    buffers = [pltpu.VMEM(shape, F32) for shape in scratch]
    if copies:
        buffers.append(pltpu.SemaphoreType.DMA((copies,)))
    return pl.pallas_call(
        kernel,
        out_shape=[jax.ShapeDtypeStruct(shape, F32) for shape in outs],
        in_specs=[SMEM] * n_scalars + [VMEM] * n_in + [ANY] * n_any,
        out_specs=[ANY if any_out else VMEM] * len(outs),
        scratch_shapes=buffers,
        compiler_params=pltpu.CompilerParams(vmem_limit_bytes=megabytes * 2**20),
        cost_estimate=pl.CostEstimate(flops=flops, bytes_accessed=moved, transcendentals=0),
        name=name,
    )


def exact(a, b, ca=1, cb=0):
    return lax.dot_general(
        a,
        b,
        (((ca,), (cb,)), ((), ())),
        precision=lax.Precision.HIGHEST,
        preferred_element_type=F32,
    )


def split(a):
    high = a.astype(jnp.bfloat16)
    return high, (a - high.astype(F32)).astype(jnp.bfloat16)


def product(a, b, ca=1, cb=0):
    def one(x, y):
        return lax.dot_general(x, y, (((ca,), (cb,)), ((), ())), preferred_element_type=F32)

    return one(a[0], b[0]) + (one(a[0], b[1]) + one(a[1], b[0]))


def linear_tile(ref, t):
    return jnp.concatenate([ref[pl.ds(t * 2 + half, NB, TR * 2), :] for half in range(2)], axis=1)


SPAN = CHUNK * TC * 2 + 4 * SHARE


def gathered_tile(ref, u):
    return jnp.concatenate(
        [
            jnp.concatenate(
                [ref[pl.ds(k * SPAN + u * 2 + half, CHUNK, TC * 2), :] for k in range(N_ROW)], axis=0
            )
            for half in range(2)
        ],
        axis=1,
    )


def matrix_rows(t, u, half):
    return pl.ds((t * NB) * TC * 2 + u * 2 + half, NB, TC * 2)


def matrix_tile(ref, t, u):
    return jnp.concatenate([ref[matrix_rows(t, u, half), :] for half in range(2)], axis=1)


def gram_kernel(place, own_ref, early_ref, late_ref, panel_ref, out_ref):
    total = jnp.zeros((SHARE, NB), F32)
    for piece in range(TR * 2):
        total += exact(
            own_ref[pl.ds(piece, SHARE, TR * 2), :], panel_ref[pl.ds(piece, NB, TR * 2), :], 1, 1
        )
    half_chunk = SHARE * TC * 2
    out_ref[:half_chunk, :] = early_ref[...]
    out_ref[half_chunk : 2 * half_chunk, :] = late_ref[...]
    for half in range(2):
        at = 2 * half_chunk + half * SHARE
        out_ref[pl.ds(at, SHARE), :] = total[:, half * LANES : (half + 1) * LANES]
        top = own_ref[pl.ds(half, SHARE, TR * 2), :]
        out_ref[pl.ds(at + 2 * SHARE, SHARE), :] = jnp.where(place[0] == 0, top, 0.0)


def gathered_columns(g_ref, quarters):
    return jnp.concatenate(
        [
            jnp.concatenate(
                [g_ref[pl.ds((4 * k + q) * SHARE, SHARE), :] for k in range(N_COL)], axis=0
            )
            for q in quarters
        ],
        axis=1,
    )


def stacked(a, b):
    def three(x):
        high = x.astype(jnp.bfloat16)
        x = x - high.astype(F32)
        mid = x.astype(jnp.bfloat16)
        return high, mid, (x - mid.astype(F32)).astype(jnp.bfloat16)

    a1, a2, a3 = three(a)
    b1, b2, b3 = three(b)
    return lax.dot_general(
        jnp.concatenate([a1, a1, a1, a2, a2, a3], axis=0),
        jnp.concatenate([b1, b2, b3, b1, b2, b1], axis=0),
        (((0,), (0,)), ((), ())),
        preferred_element_type=F32,
    )


def block_iotas():
    rows = lax.broadcasted_iota(jnp.int32, (BS, LANES), 0)
    lanes = lax.broadcasted_iota(jnp.int32, (BS, LANES), 1)
    wide = lax.broadcasted_iota(jnp.int32, (BS, NB), 1)
    return rows, lanes, wide


def turn(a_ref, base, row):
    a_ref[: NB - BS, :] = pltpu.roll(base[BS:], NB - BS, 1)
    a_ref[NB - BS :, :] = pltpu.roll(row, NB - BS, 1)


def unturned(value, a_ref, row_ref):
    turned = pltpu.roll(value, BS, 1)
    a_ref[:BS, :] = turned[NB - BS :]
    a_ref[BS:, :] = turned[: NB - BS]
    row_ref[...] = turned[NB - BS :]


def lane_spread(first):
    return [jnp.broadcast_to(first[:, k : k + 1], (BS, LANES)) for k in range(BS)]


def cholesky(g_ref, band_ref, linv_ref, upper_ref, a_ref, u_ref, row_ref, multiplier_ref):
    rows, lanes, wide = block_iotas()
    full_row, full_col = ordering()
    unturned(gathered_columns(g_ref, (0, 1)), a_ref, row_ref)
    multiplier_ref[...] = jnp.zeros((BS, NB), F32)

    def step_of(step, carry):
        left = NB - BS * step
        begun = step > 0
        a, last, multiplier = a_ref[...], row_ref[...], multiplier_ref[...]
        top = jnp.where((wide < BS) & begun, 0.0, a[BS : 2 * BS])
        top = pltpu.roll(top - stacked(multiplier[:, BS : 2 * BS], last), NB - BS, 1)
        first, second = top[:, :LANES], top[:, LANES:]
        heads = lane_spread(first)
        inner = (rows == lanes).astype(F32)
        pivots = jnp.ones((BS, LANES), F32)
        for j in range(BS):
            pivot = heads[j][j : j + 1]
            factor = jnp.where(rows > j, heads[j], 0.0) * (1.0 / pivot)
            pivots = jnp.where(rows == j, pivot, pivots)
            for k in range(j + 1, BS):
                heads[k] = heads[k] - factor * heads[k][j : j + 1]
            first = first - factor * first[j : j + 1]
            second = second - factor * second[j : j + 1]
            inner = inner - factor * inner[j : j + 1]
        scale = lax.rsqrt(pivots)
        scale = scale * (1.5 - 0.5 * pivots * scale * scale)
        first, second, inner = first * scale, second * scale, inner * scale
        upper = jnp.concatenate([jnp.where(lanes >= rows, first, 0.0), second], axis=1)
        upper = jnp.where(wide < left, upper, 0.0)
        u_ref[pl.ds(pl.multiple_of(step * BS, BS), BS), :] = pltpu.roll(upper, step * BS, 1)
        row_ref[...] = jnp.concatenate([jnp.where(lanes < BS, inner, first), second], axis=1)
        multiplier_ref[...] = jnp.where(wide >= BS, upper, 0.0)
        kept = jnp.where((full_col < BS) & (full_row < left + BS) & begun, 0.0, a)
        turn(a_ref, kept - stacked(multiplier, last), last)
        return carry

    lax.fori_loop(0, NB // BS, step_of, 0)
    turn(a_ref, a_ref[...], row_ref[...])
    linv_ref[...] = jnp.where(full_col <= full_row, a_ref[...], 0.0)
    band_ref[...] = -u_ref[...]
    upper_ref[...] = u_ref[...]


def reflector_factor(g_ref, linv_ref, refl_ref, a_ref, row_ref):
    rows, lanes, _ = block_iotas()
    full_row, full_col = ordering()
    top_block = exact(linv_ref[...], gathered_columns(g_ref, (2, 3)))
    unturned(top_block + (full_row == full_col).astype(F32), a_ref, row_ref)

    def step_of(step, carry):
        begun = step > 0
        a, last = a_ref[...], row_ref[...]
        kept = jnp.where((full_col < BS) & begun, 0.0, a)
        column = jnp.where(begun, a[:, :BS], 0.0)
        top = pltpu.roll(kept[BS : 2 * BS] - exact(column[BS : 2 * BS], last), NB - BS, 1)
        first, second = top[:, :LANES], top[:, LANES:]
        heads = lane_spread(first)
        first = jnp.where(lanes < BS, (rows == lanes).astype(F32), first)
        for j in range(BS):
            head = heads[j]
            inverse = 1.0 / head[j : j + 1]

            def put(value):
                scaled = value[j : j + 1] * inverse
                return jnp.where(rows == j, scaled, value - head * scaled)

            for k in range(j + 1, BS):
                heads[k] = put(heads[k])
            first, second = put(first), put(second)
        row_ref[...] = jnp.concatenate([first, second], axis=1)
        turn(a_ref, kept - exact(column, last), last)
        return carry

    lax.fori_loop(0, NB // BS, step_of, 0)
    a, last = a_ref[...], row_ref[...]
    turn(a_ref, jnp.where(full_col < BS, 0.0, a) - exact(a[:, :BS], last), last)
    refl_ref[...] = a_ref[...]


def reflector_kernel(g_ref, linv_ref, refl_ref, both_ref, a_ref, row_ref):
    reflector_factor(g_ref, linv_ref, refl_ref, a_ref, row_ref)
    both_ref[...] = product(split(refl_ref[...]), split(linv_ref[...]), 0, 0)


def tile_place(place, t, u):
    return t * N_ROW + place[0], u * N_COL + place[1]


def ordering():
    r = lax.broadcasted_iota(jnp.int32, (NB, NB), 0)
    c = lax.broadcasted_iota(jnp.int32, (NB, NB), 1)
    return r, c


def mirror_kernel(place, panel_ref, matrix_ref, keep_ref, send_ref, sum_ref):
    sum_ref[...] = jnp.zeros((NB, TC * NB), F32)
    for t in range(TR):
        rows = split(linear_tile(panel_ref, t))
        for u in range(TC):
            here = pl.ds(u * NB, NB)
            i, j = tile_place(place, t, u)

            @pl.when(i > j)
            def _():
                sum_ref[:, here] += product(rows, split(matrix_tile(matrix_ref, t, u)))

            @pl.when(i == j)
            def _():
                r, c = ordering()
                tile = jnp.where(r > c, matrix_tile(matrix_ref, t, u), 0.0)
                sum_ref[:, here] += product(rows, split(tile))

    for parity in range(2):

        @pl.when(place[0] % 2 == parity)
        def _():
            for k in range(N_ROW // 2):
                at = pl.ds(k * CHUNK, CHUNK)
                keep_ref[at, :] = sum_ref[pl.ds((2 * k + parity) * CHUNK, CHUNK), :]
                send_ref[at, :] = sum_ref[pl.ds((2 * k + 1 - parity) * CHUNK, CHUNK), :]


def row_copies(matrix_hbm, matrix_ref, sems, first):
    rows = matrix_ref.shape[0] // TR
    return [
        pltpu.make_async_copy(
            matrix_hbm.at[pl.ds(t * rows, rows)], matrix_ref.at[pl.ds(t * rows, rows)],
            sems.at[first + t],
        )
        for t in range(TR)
    ]


def symmetric_kernel(
    place, upper_ref, matrix_ref, panel_hbm, out_hbm, panel_ref, out_ref, sems
):
    panel_copy = pltpu.make_async_copy(panel_hbm, panel_ref, sems.at[0])
    panel_copy.start()
    out_copies = []
    factor = jnp.transpose(upper_ref[...])
    out_ref[...] = jnp.zeros((NB, TR * NB), F32)
    panel_copy.wait()
    cols = []
    for u in range(TC):
        value = gathered_tile(panel_ref, u)
        if u == 0:
            value = value + jnp.where(place[1] == 0, factor, 0.0)
        cols.append(split(value))
    for t in range(TR):
        here = pl.ds(t * NB, NB)
        for u in range(TC):
            i, j = tile_place(place, t, u)

            @pl.when(i > j)
            def _():
                out_ref[:, here] += product(cols[u], split(matrix_tile(matrix_ref, t, u)), 1, 1)

            @pl.when(i == j)
            def _():
                r, c = ordering()
                tile = jnp.where(r >= c, matrix_tile(matrix_ref, t, u), 0.0)
                out_ref[:, here] += product(cols[u], split(tile), 1, 1)

        if t == 0:

            @pl.when((place[0] == 0) & (place[1] == 0))
            def _():
                r, c = ordering()
                tile = jnp.where(r > c, matrix_tile(matrix_ref, 0, 0), 0.0)
                out_ref[:, here] += product(split(factor), split(tile))

        out_copies.append(
            pltpu.make_async_copy(out_ref.at[:, here], out_hbm.at[:, here], sems.at[1 + t])
        )
        out_copies[t].start()
    for copy in out_copies:
        copy.wait()


def vectors_kernel(
    place, linv_ref, panel_rows_ref, panel_cols_ref, rows_ref, cols_ref, vectors_ref,
):
    linv = split(linv_ref[...])
    r, c = ordering()
    eye = (r == c).astype(F32)
    for u in range(TC):
        value = product(linv, split(gathered_tile(panel_cols_ref, u)))
        if u == 0:
            value = value + jnp.where(place[1] == 0, eye, 0.0)
        cols_ref[:, pl.ds(u * NB, NB)] = value
    for t in range(TR):
        value = product(linv, split(linear_tile(panel_rows_ref, t)))
        if t == 0:
            value = value + jnp.where(place[0] == 0, eye, 0.0)
        rows_ref[:, pl.ds(t * NB, NB)] = value
    mine = rows_ref[pl.ds(pl.multiple_of(place[1] * SHARE, SHARE), SHARE), :]
    for piece in range(TR * 2):
        vectors_ref[pl.ds(piece, SHARE, TR * 2), :] = mine[:, piece * LANES : (piece + 1) * LANES]


PART = (TR + 1) * SHARE
DEAL = (TC + 1 + TR) * SHARE


def share_kernel(even_ref, odd_ref, recv_hbm, rows_hbm, out_ref, recv_ref, rows_ref, sems):
    recv_copy = pltpu.make_async_copy(recv_hbm, recv_ref, sems.at[0])
    rows_copy = pltpu.make_async_copy(rows_hbm, rows_ref, sems.at[1])
    recv_copy.start()
    rows_copy.start()
    recv_copy.wait()
    total = recv_ref[pl.ds(0, SHARE), :]
    for k in range(1, N_COL):
        total = total + recv_ref[pl.ds(k * SHARE, SHARE), :]
    mirrored = [even_ref[:, :NB], odd_ref[:, :NB], even_ref[:, NB:], odd_ref[:, NB:]]
    total = total + jnp.concatenate(mirrored, axis=1)
    for t in range(TR):
        out_ref[pl.ds(t * SHARE, SHARE), :] = total[:, t * NB : (t + 1) * NB]
    rows_copy.wait()
    out_ref[pl.ds(TR * SHARE, SHARE), :] = product(split(total), split(rows_ref[...]), 1, 1)


def deal_kernel(own_ref, part_ref, out_hbm, out_ref, sems):
    curved = part_ref[pl.ds(TR * SHARE, SHARE), :]
    for r in range(1, N_ROW):
        curved = curved + part_ref[pl.ds(r * PART + TR * SHARE, SHARE), :]
    own = own_ref[: TR * SHARE, :]
    copies = []
    group = N_COL // 4
    for c in range(N_COL):
        for u in range(TC):
            t = u * (N_COL // N_ROW) + c // N_ROW
            out_ref[pl.ds(c * DEAL + u * SHARE, SHARE), :] = part_ref[
                pl.ds((c % N_ROW) * PART + t * SHARE, SHARE), :
            ]
        out_ref[pl.ds(c * DEAL + TC * SHARE, SHARE), :] = curved
        out_ref[pl.ds(c * DEAL + (TC + 1) * SHARE, TR * SHARE), :] = own
        if c % group == group - 1:
            at = pl.ds((c + 1 - group) * DEAL, group * DEAL)
            copies.append(
                pltpu.make_async_copy(out_ref.at[at], out_hbm.at[at], sems.at[len(copies)])
            )
            copies[-1].start()
    for copy in copies:
        copy.wait()


def dealt(ref, slot):
    return jnp.concatenate(
        [ref[pl.ds(c * DEAL + slot * SHARE, SHARE), :] for c in range(N_COL)], axis=0
    )


def update_kernel(
    place, both_hbm, refl_hbm, dealt_hbm, cols_hbm, rows_hbm, matrix_hbm, out_hbm,
    both_ref, refl_ref, dealt_ref, cols_ref, rows_ref, matrix_ref, out_ref, sems,
):
    pairs = (
        (both_hbm, both_ref), (refl_hbm, refl_ref), (dealt_hbm, dealt_ref),
        (cols_hbm, cols_ref), (rows_hbm, rows_ref),
    )
    copies = [
        pltpu.make_async_copy(source, target, sems.at[k])
        for k, (source, target) in enumerate(pairs)
    ]
    matrix_copies = row_copies(matrix_hbm, matrix_ref, sems, len(copies))
    out_copies = row_copies(out_ref, out_hbm, sems, len(copies) + TR)
    for copy in copies + matrix_copies:
        copy.start()
    copies[0].wait()
    both = split(both_ref[...])
    copies[1].wait()
    refl = split(refl_ref[...])
    copies[2].wait()
    curved = split(product(both, split(dealt(dealt_ref, TC))))
    half_mixed = split(0.5 * product(curved, refl))
    copies[3].wait()
    sides = []
    for u in range(TC):
        vectors = split(cols_ref[:, pl.ds(u * NB, NB)])
        update = product(both, split(dealt(dealt_ref, u))) - product(half_mixed, vectors)
        sides.append((vectors, split(update)))
    copies[4].wait()
    for t in range(TR):
        here = pl.ds(t * NB, NB)
        vectors = split(rows_ref[:, here])
        update = split(
            product(both, split(dealt(dealt_ref, TC + 1 + t))) - product(half_mixed, vectors)
        )
        for u in range(TC):
            i, j = tile_place(place, t, u)
            if u == 0:
                matrix_copies[t].wait()

            @pl.when(i >= j)
            def _():
                change = product(vectors, sides[u][1], 0, 0) + product(update, sides[u][0], 0, 0)
                value = matrix_tile(matrix_ref, t, u) - change
                r, c = ordering()
                value = jnp.where((r >= c) | (i > j), value, 0.0)
                for half in range(2):
                    out_ref[matrix_rows(t, u, half), :] = value[:, half * LANES : (half + 1) * LANES]

            @pl.when(i < j)
            def _():
                for half in range(2):
                    out_ref[matrix_rows(t, u, half), :] = jnp.zeros((NB, LANES), F32)

        out_copies[t].start()
    for copy in out_copies:
        copy.wait()


def spread(value, axis, count):
    return lax.all_to_all(jnp.tile(value, (count, 1)), axis, 0, 0, tiled=True)


def routes():
    one, two = [], []
    for r in range(N_ROW):
        for c in range(N_COL):
            near = (c // 2) * N_COL + r
            far = near + N_ROW
            one.append((r * N_COL + c, far if c % 2 else near))
            two.append((r * N_COL + c, near if c % 2 else far))
    return one, two


def to_cols(even, odd, col_index):
    one, two = routes()
    flip, low = col_index % 2 == 1, col_index < N_ROW
    first = lax.ppermute(jnp.where(flip, odd, even), ("row", "col"), one)
    second = lax.ppermute(jnp.where(flip, even, odd), ("row", "col"), two)
    return jnp.where(low, first, second), jnp.where(low, second, first)


def to_rows(early, late, col_index):
    one, two = ([(there, here) for here, there in route] for route in routes())
    flip, low = col_index % 2 == 1, col_index < N_ROW
    first = lax.ppermute(jnp.where(low, early, late), ("row", "col"), one)
    second = lax.ppermute(jnp.where(low, late, early), ("row", "col"), two)
    return jnp.where(flip, second, first), jnp.where(flip, first, second)


def body(matrix, panel_t):
    row_index = lax.axis_index("row")
    col_index = lax.axis_index("col")
    place = jnp.stack([row_index, col_index]).astype(jnp.int32)
    stored = matrix.reshape(TR * NB * TC * 2, LANES)
    own = panel_t.reshape(SHARE * TR * 2, LANES)

    with jax.named_scope("panel"):
        by_tile = own.reshape(SHARE, TR, 2, LANES)
        chunk = to_cols(
            by_tile[:, 0::2].reshape(-1, LANES), by_tile[:, 1::2].reshape(-1, LANES), col_index
        )
        panel_rows, chunk = lax.optimization_barrier((spread(own, "col", N_COL), chunk))
    with jax.named_scope("gram"):
        (payload,) = call(
            gram_kernel, [(SPAN, LANES)], n_scalars=1, n_in=4, name="gram", moved=1 << 20
        )(place, own, *chunk, panel_rows)
        panel_cols = lax.all_gather(payload, "row", tiled=True)
        summed = panel_cols.reshape(N_ROW, SPAN, LANES)[:, CHUNK * TC * 2 :].sum(0)
        gram = spread(summed, "col", N_COL)
    with jax.named_scope("mirror"):
        keep, send = call(
            mirror_kernel, [(NB // 2, TC * NB)] * 2, scratch=[(NB, TC * NB)], n_scalars=1, n_in=2,
            name="mirror", moved=4 << 20,
        )(place, panel_rows, stored)
        mirror = keep + lax.ppermute(send, "row", [(r, r ^ 1) for r in range(N_ROW)])
        gram, mirror = lax.optimization_barrier((gram, mirror))
        parities = [list(range(parity, N_ROW, 2)) for parity in range(2)]
        mirror = lax.all_to_all(mirror, "row", 0, 0, axis_index_groups=parities, tiled=True)
        from_cols = mirror.reshape(N_ROW // 2, CHUNK, TC * NB).sum(0)
    with jax.named_scope("factor"):
        band, linv, upper = call(
            cholesky,
            [(NB, NB)] * 3,
            scratch=[(NB, NB)] * 2 + [(BS, NB)] * 2,
            n_in=1,
            name="cholesky",
            flops=5 * 10**9,
            moved=40 << 20,
        )(gram)
    with jax.named_scope("symmetric"):
        (row_terms,) = call(
            symmetric_kernel, [(NB, TR * NB)],
            scratch=[(N_ROW * SPAN, LANES), (NB, TR * NB)],
            n_scalars=1, n_in=2, n_any=1, any_out=True, copies=1 + TR,
            name="symmetric", moved=4 << 20,
        )(place, upper, stored, panel_cols)
    with jax.named_scope("vectors"):
        rows, cols, vectors = call(
            vectors_kernel,
            [(NB, TR * NB), (NB, TC * NB), (SHARE * TR * 2, LANES)],
            n_scalars=1,
            n_in=3,
            name="vectors",
            moved=4 << 20,
        )(place, linv, panel_rows, panel_cols)
    with jax.named_scope("sums"):
        received = lax.all_to_all(row_terms, "col", 0, 0, tiled=True)
        even, odd = to_rows(from_cols[:SHARE], from_cols[SHARE:], col_index)
        (payload,) = call(
            share_kernel, [(PART, NB)], scratch=[(NB, TR * NB)] * 2, n_in=2, n_any=2, copies=2,
            name="share", moved=2 << 20, megabytes=60,
        )(even, odd, received, rows)
        parts = lax.all_gather(payload, "row", tiled=True)
    with jax.named_scope("deal"):
        (deal,) = call(
            deal_kernel, [(N_COL * DEAL, NB)], scratch=[(N_COL * DEAL, NB)], n_in=2, any_out=True,
            copies=4, name="deal", moved=3 << 20,
        )(payload, parts)
        deal, gram, linv = lax.optimization_barrier((deal, gram, linv))
        deal = lax.all_to_all(deal, "col", 0, 0, tiled=True)
    with jax.named_scope("reflector"):
        reflector, both = call(
            reflector_kernel,
            [(NB, NB)] * 2,
            scratch=[(NB, NB), (BS, NB)],
            n_in=2,
            name="reflector",
            flops=5 * 10**9,
            moved=40 << 20,
        )(gram, linv)
    with jax.named_scope("update"):
        (updated,) = call(
            update_kernel,
            [(TR * NB * TC * 2, LANES)],
            scratch=[
                (NB, NB),
                (NB, NB),
                (N_COL * DEAL, NB),
                (NB, TC * NB),
                (NB, TR * NB),
                (TR * NB * TC * 2, LANES),
                (TR * NB * TC * 2, LANES),
            ],
            n_scalars=1,
            n_in=0,
            n_any=6,
            any_out=True,
            copies=5 + 2 * TR,
            megabytes=60,
            name="update",
            moved=8 << 20,
        )(place, both, reflector, deal, cols, rows, stored)
    return (updated.reshape(matrix.shape), vectors.reshape(panel_t.shape), band, reflector)


def solution(mesh):
    placed = (P(None, "row", None, None, "col", None), P("col", None, "row", None))
    return jax.shard_map(
        body,
        mesh=mesh,
        in_specs=placed,
        out_specs=(P(None, "row", None, None, "col", None), P("col", None, "row", None), P(), P()),
        check_vma=False,
    )
```

```python
import jax
import jax.numpy as jnp
from jax import lax
from jax.experimental import pallas as pl
from jax.experimental.pallas import tpu as pltpu
from jax.sharding import PartitionSpec as P

NB = 256
TR = 4
TC = 2
N_ROW = 16
N_COL = 32
LANES = 128
BS = 16
SHARE = NB // N_COL
CHUNK = NB // N_ROW
PAIRS = [(r, r ^ 1) for r in range(N_ROW)]
PARITIES = [list(range(parity, N_ROW, 2)) for parity in range(2)]
F32 = jnp.float32
VMEM = pl.BlockSpec(memory_space=pltpu.VMEM)
SMEM = pl.BlockSpec(memory_space=pltpu.SMEM)


ANY = pl.BlockSpec(memory_space=pl.ANY)


def call(
    kernel, outs, scratch=(), n_scalars=0, n_in=1, n_any=0, any_out=False, copies=0,
    name=None, flops=0, moved=0, megabytes=40,
):
    buffers = [pltpu.VMEM(shape, F32) for shape in scratch]
    if copies:
        buffers.append(pltpu.SemaphoreType.DMA((copies,)))
    return pl.pallas_call(
        kernel,
        out_shape=[jax.ShapeDtypeStruct(shape, F32) for shape in outs],
        in_specs=[SMEM] * n_scalars + [VMEM] * n_in + [ANY] * n_any,
        out_specs=[ANY if any_out else VMEM] * len(outs),
        scratch_shapes=buffers,
        compiler_params=pltpu.CompilerParams(vmem_limit_bytes=megabytes * 2**20),
        cost_estimate=pl.CostEstimate(flops=flops, bytes_accessed=moved, transcendentals=0),
        name=name,
    )


def exact(a, b, ca=1, cb=0):
    return lax.dot_general(
        a,
        b,
        (((ca,), (cb,)), ((), ())),
        precision=lax.Precision.HIGHEST,
        preferred_element_type=F32,
    )


def split(a):
    high = a.astype(jnp.bfloat16)
    return high, (a - high.astype(F32)).astype(jnp.bfloat16)


def product(a, b, ca=1, cb=0):
    def one(x, y):
        return lax.dot_general(x, y, (((ca,), (cb,)), ((), ())), preferred_element_type=F32)

    return one(a[0], b[0]) + (one(a[0], b[1]) + one(a[1], b[0]))


def linear_tile(ref, t):
    return jnp.concatenate([ref[pl.ds(t * 2 + half, NB, TR * 2), :] for half in range(2)], axis=1)


SPAN = CHUNK * TC * 2 + 4 * SHARE


def gathered_tile(ref, u):
    return jnp.concatenate(
        [
            jnp.concatenate(
                [ref[pl.ds(k * SPAN + u * 2 + half, CHUNK, TC * 2), :] for k in range(N_ROW)], axis=0
            )
            for half in range(2)
        ],
        axis=1,
    )


def matrix_rows(t, u, half):
    return pl.ds((t * NB) * TC * 2 + u * 2 + half, NB, TC * 2)


def matrix_tile(ref, t, u):
    return jnp.concatenate([ref[matrix_rows(t, u, half), :] for half in range(2)], axis=1)


def gram_kernel(place, own_ref, early_ref, late_ref, panel_ref, out_ref):
    total = jnp.zeros((SHARE, NB), F32)
    for piece in range(TR * 2):
        total += exact(
            own_ref[pl.ds(piece, SHARE, TR * 2), :], panel_ref[pl.ds(piece, NB, TR * 2), :], 1, 1
        )
    half_chunk = SHARE * TC * 2
    out_ref[:half_chunk, :] = early_ref[...]
    out_ref[half_chunk : 2 * half_chunk, :] = late_ref[...]
    for half in range(2):
        at = 2 * half_chunk + half * SHARE
        out_ref[pl.ds(at, SHARE), :] = total[:, half * LANES : (half + 1) * LANES]
        top = own_ref[pl.ds(half, SHARE, TR * 2), :]
        out_ref[pl.ds(at + 2 * SHARE, SHARE), :] = jnp.where(place[0] == 0, top, 0.0)


def gathered_columns(g_ref, quarters):
    return jnp.concatenate(
        [
            jnp.concatenate(
                [g_ref[pl.ds((4 * k + q) * SHARE, SHARE), :] for k in range(N_COL)], axis=0
            )
            for q in quarters
        ],
        axis=1,
    )


def stacked(a, b):
    def three(x):
        high = x.astype(jnp.bfloat16)
        x = x - high.astype(F32)
        mid = x.astype(jnp.bfloat16)
        return high, mid, (x - mid.astype(F32)).astype(jnp.bfloat16)

    a1, a2, a3 = three(a)
    b1, b2, b3 = three(b)
    return lax.dot_general(
        jnp.concatenate([a1, a1, a1, a2, a2, a3], axis=0),
        jnp.concatenate([b1, b2, b3, b1, b2, b1], axis=0),
        (((0,), (0,)), ((), ())),
        preferred_element_type=F32,
    )


def block_iotas():
    rows = lax.broadcasted_iota(jnp.int32, (BS, LANES), 0)
    lanes = lax.broadcasted_iota(jnp.int32, (BS, LANES), 1)
    wide = lax.broadcasted_iota(jnp.int32, (BS, NB), 1)
    return rows, lanes, wide


def turn(a_ref, base, row):
    a_ref[: NB - BS, :] = pltpu.roll(base[BS:], NB - BS, 1)
    a_ref[NB - BS :, :] = pltpu.roll(row, NB - BS, 1)


def unturned(value, a_ref, row_ref):
    turned = pltpu.roll(value, BS, 1)
    a_ref[:BS, :] = turned[NB - BS :]
    a_ref[BS:, :] = turned[: NB - BS]
    row_ref[...] = turned[NB - BS :]


def lane_spread(first):
    return [jnp.broadcast_to(first[:, k : k + 1], (BS, LANES)) for k in range(BS)]


def cholesky(g_ref, band_ref, linv_ref, upper_ref, a_ref, u_ref, row_ref, multiplier_ref):
    rows, lanes, wide = block_iotas()
    full_row, full_col = ordering()
    unturned(gathered_columns(g_ref, (0, 1)), a_ref, row_ref)
    multiplier_ref[...] = jnp.zeros((BS, NB), F32)

    def step_of(step, carry):
        left = NB - BS * step
        begun = step > 0
        a, last, multiplier = a_ref[...], row_ref[...], multiplier_ref[...]
        top = jnp.where((wide < BS) & begun, 0.0, a[BS : 2 * BS])
        top = pltpu.roll(top - stacked(multiplier[:, BS : 2 * BS], last), NB - BS, 1)
        first, second = top[:, :LANES], top[:, LANES:]
        heads = lane_spread(first)
        inner = (rows == lanes).astype(F32)
        pivots = jnp.ones((BS, LANES), F32)
        for j in range(BS):
            pivot = heads[j][j : j + 1]
            factor = jnp.where(rows > j, heads[j], 0.0) * (1.0 / pivot)
            pivots = jnp.where(rows == j, pivot, pivots)
            for k in range(j + 1, BS):
                heads[k] = heads[k] - factor * heads[k][j : j + 1]
            first = first - factor * first[j : j + 1]
            second = second - factor * second[j : j + 1]
            inner = inner - factor * inner[j : j + 1]
        scale = lax.rsqrt(pivots)
        scale = scale * (1.5 - 0.5 * pivots * scale * scale)
        first, second, inner = first * scale, second * scale, inner * scale
        upper = jnp.concatenate([jnp.where(lanes >= rows, first, 0.0), second], axis=1)
        upper = jnp.where(wide < left, upper, 0.0)
        u_ref[pl.ds(pl.multiple_of(step * BS, BS), BS), :] = pltpu.roll(upper, step * BS, 1)
        row_ref[...] = jnp.concatenate([jnp.where(lanes < BS, inner, first), second], axis=1)
        multiplier_ref[...] = jnp.where(wide >= BS, upper, 0.0)
        kept = jnp.where((full_col < BS) & (full_row < left + BS) & begun, 0.0, a)
        turn(a_ref, kept - stacked(multiplier, last), last)
        return carry

    lax.fori_loop(0, NB // BS, step_of, 0)
    turn(a_ref, a_ref[...], row_ref[...])
    linv_ref[...] = jnp.where(full_col <= full_row, a_ref[...], 0.0)
    band_ref[...] = -u_ref[...]
    upper_ref[...] = u_ref[...]


def reflector_factor(g_ref, linv_ref, refl_ref, a_ref, row_ref):
    rows, lanes, _ = block_iotas()
    full_row, full_col = ordering()
    top_block = exact(linv_ref[...], gathered_columns(g_ref, (2, 3)))
    unturned(top_block + (full_row == full_col).astype(F32), a_ref, row_ref)

    def step_of(step, carry):
        begun = step > 0
        a, last = a_ref[...], row_ref[...]
        kept = jnp.where((full_col < BS) & begun, 0.0, a)
        column = jnp.where(begun, a[:, :BS], 0.0)
        top = pltpu.roll(kept[BS : 2 * BS] - exact(column[BS : 2 * BS], last), NB - BS, 1)
        first, second = top[:, :LANES], top[:, LANES:]
        heads = lane_spread(first)
        first = jnp.where(lanes < BS, (rows == lanes).astype(F32), first)
        for j in range(BS):
            head = heads[j]
            inverse = 1.0 / head[j : j + 1]

            def put(value):
                scaled = value[j : j + 1] * inverse
                return jnp.where(rows == j, scaled, value - head * scaled)

            for k in range(j + 1, BS):
                heads[k] = put(heads[k])
            first, second = put(first), put(second)
        row_ref[...] = jnp.concatenate([first, second], axis=1)
        turn(a_ref, kept - exact(column, last), last)
        return carry

    lax.fori_loop(0, NB // BS, step_of, 0)
    a, last = a_ref[...], row_ref[...]
    turn(a_ref, jnp.where(full_col < BS, 0.0, a) - exact(a[:, :BS], last), last)
    refl_ref[...] = a_ref[...]


def reflector_kernel(g_ref, linv_ref, refl_ref, both_ref, a_ref, row_ref):
    reflector_factor(g_ref, linv_ref, refl_ref, a_ref, row_ref)
    both_ref[...] = product(split(refl_ref[...]), split(linv_ref[...]), 0, 0)


def tile_place(place, t, u):
    return t * N_ROW + place[0], u * N_COL + place[1]


def ordering():
    r = lax.broadcasted_iota(jnp.int32, (NB, NB), 0)
    c = lax.broadcasted_iota(jnp.int32, (NB, NB), 1)
    return r, c


def mirror_kernel(place, panel_ref, matrix_ref, keep_ref, send_ref, sum_ref):
    sum_ref[...] = jnp.zeros((NB, TC * NB), F32)
    for t in range(TR):
        rows = split(linear_tile(panel_ref, t))
        for u in range(TC):
            here = pl.ds(u * NB, NB)
            i, j = tile_place(place, t, u)

            @pl.when(i > j)
            def _():
                sum_ref[:, here] += product(rows, split(matrix_tile(matrix_ref, t, u)))

            @pl.when(i == j)
            def _():
                r, c = ordering()
                tile = jnp.where(r > c, matrix_tile(matrix_ref, t, u), 0.0)
                sum_ref[:, here] += product(rows, split(tile))

    for parity in range(2):

        @pl.when(place[0] % 2 == parity)
        def _():
            for k in range(N_ROW // 2):
                at = pl.ds(k * CHUNK, CHUNK)
                keep_ref[at, :] = sum_ref[pl.ds((2 * k + parity) * CHUNK, CHUNK), :]
                send_ref[at, :] = sum_ref[pl.ds((2 * k + 1 - parity) * CHUNK, CHUNK), :]


def row_copies(matrix_hbm, matrix_ref, sems, first):
    rows = matrix_ref.shape[0] // TR
    return [
        pltpu.make_async_copy(
            matrix_hbm.at[pl.ds(t * rows, rows)], matrix_ref.at[pl.ds(t * rows, rows)],
            sems.at[first + t],
        )
        for t in range(TR)
    ]


def symmetric_kernel(
    place, upper_ref, matrix_ref, panel_hbm, out_hbm, panel_ref, out_ref, sems
):
    panel_copy = pltpu.make_async_copy(panel_hbm, panel_ref, sems.at[0])
    panel_copy.start()
    out_copies = []
    factor = jnp.transpose(upper_ref[...])
    out_ref[...] = jnp.zeros((NB, TR * NB), F32)
    panel_copy.wait()
    cols = []
    for u in range(TC):
        value = gathered_tile(panel_ref, u)
        if u == 0:
            value = value + jnp.where(place[1] == 0, factor, 0.0)
        cols.append(split(value))
    for t in range(TR):
        here = pl.ds(t * NB, NB)
        for u in range(TC):
            i, j = tile_place(place, t, u)

            @pl.when(i > j)
            def _():
                out_ref[:, here] += product(cols[u], split(matrix_tile(matrix_ref, t, u)), 1, 1)

            @pl.when(i == j)
            def _():
                r, c = ordering()
                tile = jnp.where(r >= c, matrix_tile(matrix_ref, t, u), 0.0)
                out_ref[:, here] += product(cols[u], split(tile), 1, 1)

        if t == 0:

            @pl.when((place[0] == 0) & (place[1] == 0))
            def _():
                r, c = ordering()
                tile = jnp.where(r > c, matrix_tile(matrix_ref, 0, 0), 0.0)
                out_ref[:, here] += product(split(factor), split(tile))

        out_copies.append(
            pltpu.make_async_copy(out_ref.at[:, here], out_hbm.at[:, here], sems.at[1 + t])
        )
        out_copies[t].start()
    for copy in out_copies:
        copy.wait()


def vectors_kernel(
    place, linv_ref, panel_rows_ref, panel_cols_ref, rows_ref, cols_ref, vectors_ref,
):
    linv = split(linv_ref[...])
    r, c = ordering()
    eye = (r == c).astype(F32)
    for u in range(TC):
        value = product(linv, split(gathered_tile(panel_cols_ref, u)))
        if u == 0:
            value = value + jnp.where(place[1] == 0, eye, 0.0)
        cols_ref[:, pl.ds(u * NB, NB)] = value
    for t in range(TR):
        value = product(linv, split(linear_tile(panel_rows_ref, t)))
        if t == 0:
            value = value + jnp.where(place[0] == 0, eye, 0.0)
        rows_ref[:, pl.ds(t * NB, NB)] = value
    mine = rows_ref[pl.ds(pl.multiple_of(place[1] * SHARE, SHARE), SHARE), :]
    for piece in range(TR * 2):
        vectors_ref[pl.ds(piece, SHARE, TR * 2), :] = mine[:, piece * LANES : (piece + 1) * LANES]


PART = (TR + 1) * SHARE
DEAL = (TC + 1 + TR) * SHARE


def share_kernel(even_ref, odd_ref, recv_hbm, rows_hbm, out_ref, recv_ref, rows_ref, sems):
    recv_copy = pltpu.make_async_copy(recv_hbm, recv_ref, sems.at[0])
    rows_copy = pltpu.make_async_copy(rows_hbm, rows_ref, sems.at[1])
    recv_copy.start()
    rows_copy.start()
    recv_copy.wait()
    total = recv_ref[pl.ds(0, SHARE), :]
    for k in range(1, N_COL):
        total = total + recv_ref[pl.ds(k * SHARE, SHARE), :]
    mirrored = [even_ref[:, :NB], odd_ref[:, :NB], even_ref[:, NB:], odd_ref[:, NB:]]
    total = total + jnp.concatenate(mirrored, axis=1)
    for t in range(TR):
        out_ref[pl.ds(t * SHARE, SHARE), :] = total[:, t * NB : (t + 1) * NB]
    rows_copy.wait()
    out_ref[pl.ds(TR * SHARE, SHARE), :] = product(split(total), split(rows_ref[...]), 1, 1)


def deal_kernel(place, own_ref, same_ref, other_ref, out_hbm, out_ref, sems):
    curved = jnp.zeros((SHARE, NB), F32)
    for k in range(N_ROW // 2):
        at = pl.ds(k * PART + TR * SHARE, SHARE)
        curved = curved + (same_ref[at, :] + other_ref[at, :])
    own = own_ref[: TR * SHARE, :]
    parity = place[0] % 2
    copies = []
    group = N_COL // 4
    for c in range(N_COL):
        for u in range(TC):
            t = u * (N_COL // N_ROW) + c // N_ROW
            r = c % N_ROW
            at = pl.ds((r // 2) * PART + t * SHARE, SHARE)
            out_ref[pl.ds(c * DEAL + u * SHARE, SHARE), :] = jnp.where(
                parity == r % 2, same_ref[at, :], other_ref[at, :]
            )
        out_ref[pl.ds(c * DEAL + TC * SHARE, SHARE), :] = curved
        out_ref[pl.ds(c * DEAL + (TC + 1) * SHARE, TR * SHARE), :] = own
        if c % group == group - 1:
            at = pl.ds((c + 1 - group) * DEAL, group * DEAL)
            copies.append(
                pltpu.make_async_copy(out_ref.at[at], out_hbm.at[at], sems.at[len(copies)])
            )
            copies[-1].start()
    for copy in copies:
        copy.wait()


def dealt(ref, slot):
    return jnp.concatenate(
        [ref[pl.ds(c * DEAL + slot * SHARE, SHARE), :] for c in range(N_COL)], axis=0
    )


def update_kernel(
    place, both_hbm, refl_hbm, dealt_hbm, cols_hbm, rows_hbm, matrix_hbm, out_hbm,
    both_ref, refl_ref, dealt_ref, cols_ref, rows_ref, matrix_ref, out_ref, sems,
):
    pairs = (
        (both_hbm, both_ref), (refl_hbm, refl_ref), (dealt_hbm, dealt_ref),
        (cols_hbm, cols_ref), (rows_hbm, rows_ref),
    )
    copies = [
        pltpu.make_async_copy(source, target, sems.at[k])
        for k, (source, target) in enumerate(pairs)
    ]
    matrix_copies = row_copies(matrix_hbm, matrix_ref, sems, len(copies))
    out_copies = row_copies(out_ref, out_hbm, sems, len(copies) + TR)
    for copy in copies + matrix_copies:
        copy.start()
    copies[0].wait()
    both = split(both_ref[...])
    copies[1].wait()
    refl = split(refl_ref[...])
    copies[2].wait()
    curved = split(product(both, split(dealt(dealt_ref, TC))))
    half_mixed = split(0.5 * product(curved, refl))
    copies[3].wait()
    sides = []
    for u in range(TC):
        vectors = split(cols_ref[:, pl.ds(u * NB, NB)])
        update = product(both, split(dealt(dealt_ref, u))) - product(half_mixed, vectors)
        sides.append((vectors, split(update)))
    copies[4].wait()
    for t in range(TR):
        here = pl.ds(t * NB, NB)
        vectors = split(rows_ref[:, here])
        update = split(
            product(both, split(dealt(dealt_ref, TC + 1 + t))) - product(half_mixed, vectors)
        )
        for u in range(TC):
            i, j = tile_place(place, t, u)
            if u == 0:
                matrix_copies[t].wait()

            @pl.when(i >= j)
            def _():
                change = product(vectors, sides[u][1], 0, 0) + product(update, sides[u][0], 0, 0)
                value = matrix_tile(matrix_ref, t, u) - change
                r, c = ordering()
                value = jnp.where((r >= c) | (i > j), value, 0.0)
                for half in range(2):
                    out_ref[matrix_rows(t, u, half), :] = value[:, half * LANES : (half + 1) * LANES]

            @pl.when(i < j)
            def _():
                for half in range(2):
                    out_ref[matrix_rows(t, u, half), :] = jnp.zeros((NB, LANES), F32)

        out_copies[t].start()
    for copy in out_copies:
        copy.wait()


def spread(value, axis, count):
    return lax.all_to_all(jnp.tile(value, (count, 1)), axis, 0, 0, tiled=True)


def routes():
    one, two = [], []
    for r in range(N_ROW):
        for c in range(N_COL):
            near = (c // 2) * N_COL + r
            far = near + N_ROW
            one.append((r * N_COL + c, far if c % 2 else near))
            two.append((r * N_COL + c, near if c % 2 else far))
    return one, two


def to_cols(even, odd, col_index):
    one, two = routes()
    flip, low = col_index % 2 == 1, col_index < N_ROW
    first = lax.ppermute(jnp.where(flip, odd, even), ("row", "col"), one)
    second = lax.ppermute(jnp.where(flip, even, odd), ("row", "col"), two)
    return jnp.where(low, first, second), jnp.where(low, second, first)


def to_rows(early, late, col_index):
    one, two = ([(there, here) for here, there in route] for route in routes())
    flip, low = col_index % 2 == 1, col_index < N_ROW
    first = lax.ppermute(jnp.where(low, early, late), ("row", "col"), one)
    second = lax.ppermute(jnp.where(low, late, early), ("row", "col"), two)
    return jnp.where(flip, second, first), jnp.where(flip, first, second)


def body(matrix, panel_t):
    row_index = lax.axis_index("row")
    col_index = lax.axis_index("col")
    place = jnp.stack([row_index, col_index]).astype(jnp.int32)
    stored = matrix.reshape(TR * NB * TC * 2, LANES)
    own = panel_t.reshape(SHARE * TR * 2, LANES)

    with jax.named_scope("panel"):
        by_tile = own.reshape(SHARE, TR, 2, LANES)
        chunk = to_cols(
            by_tile[:, 0::2].reshape(-1, LANES), by_tile[:, 1::2].reshape(-1, LANES), col_index
        )
        panel_rows, chunk = lax.optimization_barrier((spread(own, "col", N_COL), chunk))
    with jax.named_scope("gram"):
        (payload,) = call(
            gram_kernel, [(SPAN, LANES)], n_scalars=1, n_in=4, name="gram", moved=1 << 20
        )(place, own, *chunk, panel_rows)
        panel_cols = lax.all_gather(payload, "row", tiled=True)
        summed = panel_cols.reshape(N_ROW, SPAN, LANES)[:, CHUNK * TC * 2 :].sum(0)
        gram = spread(summed, "col", N_COL)
    with jax.named_scope("mirror"):
        keep, send = call(
            mirror_kernel, [(NB // 2, TC * NB)] * 2, scratch=[(NB, TC * NB)], n_scalars=1, n_in=2,
            name="mirror", moved=4 << 20,
        )(place, panel_rows, stored)
        mirror = keep + lax.ppermute(send, "row", PAIRS)
        gram, mirror = lax.optimization_barrier((gram, mirror))
        mirror = lax.all_to_all(mirror, "row", 0, 0, axis_index_groups=PARITIES, tiled=True)
        from_cols = mirror.reshape(N_ROW // 2, CHUNK, TC * NB).sum(0)
    with jax.named_scope("factor"):
        band, linv, upper = call(
            cholesky,
            [(NB, NB)] * 3,
            scratch=[(NB, NB)] * 2 + [(BS, NB)] * 2,
            n_in=1,
            name="cholesky",
            flops=5 * 10**9,
            moved=40 << 20,
        )(gram)
    with jax.named_scope("symmetric"):
        (row_terms,) = call(
            symmetric_kernel, [(NB, TR * NB)],
            scratch=[(N_ROW * SPAN, LANES), (NB, TR * NB)],
            n_scalars=1, n_in=2, n_any=1, any_out=True, copies=1 + TR,
            name="symmetric", moved=4 << 20,
        )(place, upper, stored, panel_cols)
    with jax.named_scope("vectors"):
        rows, cols, vectors = call(
            vectors_kernel,
            [(NB, TR * NB), (NB, TC * NB), (SHARE * TR * 2, LANES)],
            n_scalars=1,
            n_in=3,
            name="vectors",
            moved=4 << 20,
        )(place, linv, panel_rows, panel_cols)
    with jax.named_scope("sums"):
        received = lax.all_to_all(row_terms, "col", 0, 0, tiled=True)
        even, odd = to_rows(from_cols[:SHARE], from_cols[SHARE:], col_index)
        (payload,) = call(
            share_kernel, [(PART, NB)], scratch=[(NB, TR * NB)] * 2, n_in=2, n_any=2, copies=2,
            name="share", moved=2 << 20,
        )(even, odd, received, rows)
        same = lax.all_to_all(
            jnp.tile(payload, (N_ROW // 2, 1)), "row", 0, 0, axis_index_groups=PARITIES, tiled=True
        )
        other = lax.ppermute(same, "row", PAIRS)
    with jax.named_scope("deal"):
        (deal,) = call(
            deal_kernel, [(N_COL * DEAL, NB)], scratch=[(N_COL * DEAL, NB)], n_scalars=1, n_in=3,
            any_out=True, copies=4, name="deal", moved=3 << 20,
        )(place, payload, same, other)
        deal, gram, linv = lax.optimization_barrier((deal, gram, linv))
        deal = lax.all_to_all(deal, "col", 0, 0, tiled=True)
    with jax.named_scope("reflector"):
        reflector, both = call(
            reflector_kernel,
            [(NB, NB)] * 2,
            scratch=[(NB, NB), (BS, NB)],
            n_in=2,
            name="reflector",
            flops=5 * 10**9,
            moved=40 << 20,
        )(gram, linv)
    with jax.named_scope("update"):
        (updated,) = call(
            update_kernel,
            [(TR * NB * TC * 2, LANES)],
            scratch=[
                (NB, NB),
                (NB, NB),
                (N_COL * DEAL, NB),
                (NB, TC * NB),
                (NB, TR * NB),
                (TR * NB * TC * 2, LANES),
                (TR * NB * TC * 2, LANES),
            ],
            n_scalars=1,
            n_in=0,
            n_any=6,
            any_out=True,
            copies=5 + 2 * TR,
            megabytes=60,
            name="update",
            moved=8 << 20,
        )(place, both, reflector, deal, cols, rows, stored)
    return (updated.reshape(matrix.shape), vectors.reshape(panel_t.shape), band, reflector)


def solution(mesh):
    placed = (P(None, "row", None, None, "col", None), P("col", None, "row", None))
    return jax.shard_map(
        body,
        mesh=mesh,
        in_specs=placed,
        out_specs=(P(None, "row", None, None, "col", None), P("col", None, "row", None), P(), P()),
        check_vma=False,
    )
```

```python
import jax
import jax.numpy as jnp
from jax import lax
from jax.experimental import pallas as pl
from jax.experimental.pallas import tpu as pltpu
from jax.sharding import PartitionSpec as P

NB = 256
TR = 4
TC = 2
N_ROW = 16
N_COL = 32
LANES = 128
BS = 16
SHARE = NB // N_COL
CHUNK = NB // N_ROW
F32 = jnp.float32
VMEM = pl.BlockSpec(memory_space=pltpu.VMEM)
SMEM = pl.BlockSpec(memory_space=pltpu.SMEM)


ANY = pl.BlockSpec(memory_space=pl.ANY)


def call(
    kernel, outs, scratch=(), n_scalars=0, n_in=1, n_any=0, any_out=False, copies=0,
    name=None, flops=0, moved=0, megabytes=40,
):
    buffers = [pltpu.VMEM(shape, F32) for shape in scratch]
    if copies:
        buffers.append(pltpu.SemaphoreType.DMA((copies,)))
    return pl.pallas_call(
        kernel,
        out_shape=[jax.ShapeDtypeStruct(shape, F32) for shape in outs],
        in_specs=[SMEM] * n_scalars + [VMEM] * n_in + [ANY] * n_any,
        out_specs=[ANY if any_out else VMEM] * len(outs),
        scratch_shapes=buffers,
        compiler_params=pltpu.CompilerParams(vmem_limit_bytes=megabytes * 2**20),
        cost_estimate=pl.CostEstimate(flops=flops, bytes_accessed=moved, transcendentals=0),
        name=name,
    )


def exact(a, b, ca=1, cb=0):
    return lax.dot_general(
        a,
        b,
        (((ca,), (cb,)), ((), ())),
        precision=lax.Precision.HIGHEST,
        preferred_element_type=F32,
    )


def split(a):
    high = a.astype(jnp.bfloat16)
    return high, (a - high.astype(F32)).astype(jnp.bfloat16)


def product(a, b, ca=1, cb=0):
    def one(x, y):
        return lax.dot_general(x, y, (((ca,), (cb,)), ((), ())), preferred_element_type=F32)

    return one(a[0], b[0]) + (one(a[0], b[1]) + one(a[1], b[0]))


def linear_tile(ref, t):
    return jnp.concatenate([ref[pl.ds(t * 2 + half, NB, TR * 2), :] for half in range(2)], axis=1)


SPAN = CHUNK * TC * 2 + 4 * SHARE


def gathered_tile(ref, u):
    return jnp.concatenate(
        [
            jnp.concatenate(
                [ref[pl.ds(k * SPAN + u * 2 + half, CHUNK, TC * 2), :] for k in range(N_ROW)], axis=0
            )
            for half in range(2)
        ],
        axis=1,
    )


def matrix_rows(t, u, half):
    return pl.ds((t * NB) * TC * 2 + u * 2 + half, NB, TC * 2)


def matrix_tile(ref, t, u):
    return jnp.concatenate([ref[matrix_rows(t, u, half), :] for half in range(2)], axis=1)


def gram_kernel(place, own_ref, early_ref, late_ref, panel_ref, out_ref):
    total = jnp.zeros((SHARE, NB), F32)
    for piece in range(TR * 2):
        total += exact(
            own_ref[pl.ds(piece, SHARE, TR * 2), :], panel_ref[pl.ds(piece, NB, TR * 2), :], 1, 1
        )
    half_chunk = SHARE * TC * 2
    out_ref[:half_chunk, :] = early_ref[...]
    out_ref[half_chunk : 2 * half_chunk, :] = late_ref[...]
    for half in range(2):
        at = 2 * half_chunk + half * SHARE
        out_ref[pl.ds(at, SHARE), :] = total[:, half * LANES : (half + 1) * LANES]
        top = own_ref[pl.ds(half, SHARE, TR * 2), :]
        out_ref[pl.ds(at + 2 * SHARE, SHARE), :] = jnp.where(place[0] == 0, top, 0.0)


def gathered_columns(g_ref, quarters):
    return jnp.concatenate(
        [
            jnp.concatenate(
                [g_ref[pl.ds((4 * k + q) * SHARE, SHARE), :] for k in range(N_COL)], axis=0
            )
            for q in quarters
        ],
        axis=1,
    )


def stacked(a, b):
    def three(x):
        high = x.astype(jnp.bfloat16)
        x = x - high.astype(F32)
        mid = x.astype(jnp.bfloat16)
        return high, mid, (x - mid.astype(F32)).astype(jnp.bfloat16)

    a1, a2, a3 = three(a)
    b1, b2, b3 = three(b)
    return lax.dot_general(
        jnp.concatenate([a1, a1, a1, a2, a2, a3], axis=0),
        jnp.concatenate([b1, b2, b3, b1, b2, b1], axis=0),
        (((0,), (0,)), ((), ())),
        preferred_element_type=F32,
    )


def block_iotas():
    rows = lax.broadcasted_iota(jnp.int32, (BS, LANES), 0)
    lanes = lax.broadcasted_iota(jnp.int32, (BS, LANES), 1)
    wide = lax.broadcasted_iota(jnp.int32, (BS, NB), 1)
    return rows, lanes, wide


def turn(a_ref, base, row):
    a_ref[: NB - BS, :] = pltpu.roll(base[BS:], NB - BS, 1)
    a_ref[NB - BS :, :] = pltpu.roll(row, NB - BS, 1)


def unturned(value, a_ref, row_ref):
    turned = pltpu.roll(value, BS, 1)
    a_ref[:BS, :] = turned[NB - BS :]
    a_ref[BS:, :] = turned[: NB - BS]
    row_ref[...] = turned[NB - BS :]


def lane_spread(first):
    return [jnp.broadcast_to(first[:, k : k + 1], (BS, LANES)) for k in range(BS)]


def cholesky(g_ref, band_ref, linv_ref, upper_ref, a_ref, u_ref, row_ref, multiplier_ref):
    rows, lanes, wide = block_iotas()
    full_row, full_col = ordering()
    unturned(gathered_columns(g_ref, (0, 1)), a_ref, row_ref)
    multiplier_ref[...] = jnp.zeros((BS, NB), F32)

    def step_of(step, carry):
        left = NB - BS * step
        begun = step > 0
        a, last, multiplier = a_ref[...], row_ref[...], multiplier_ref[...]
        top = jnp.where((wide < BS) & begun, 0.0, a[BS : 2 * BS])
        top = pltpu.roll(top - stacked(multiplier[:, BS : 2 * BS], last), NB - BS, 1)
        first, second = top[:, :LANES], top[:, LANES:]
        heads = lane_spread(first)
        inner = (rows == lanes).astype(F32)
        pivots = jnp.ones((BS, LANES), F32)
        for j in range(BS):
            pivot = heads[j][j : j + 1]
            factor = jnp.where(rows > j, heads[j], 0.0) * (1.0 / pivot)
            pivots = jnp.where(rows == j, pivot, pivots)
            for k in range(j + 1, BS):
                heads[k] = heads[k] - factor * heads[k][j : j + 1]
            first = first - factor * first[j : j + 1]
            second = second - factor * second[j : j + 1]
            inner = inner - factor * inner[j : j + 1]
        scale = lax.rsqrt(pivots)
        scale = scale * (1.5 - 0.5 * pivots * scale * scale)
        first, second, inner = first * scale, second * scale, inner * scale
        upper = jnp.concatenate([jnp.where(lanes >= rows, first, 0.0), second], axis=1)
        upper = jnp.where(wide < left, upper, 0.0)
        u_ref[pl.ds(pl.multiple_of(step * BS, BS), BS), :] = pltpu.roll(upper, step * BS, 1)
        row_ref[...] = jnp.concatenate([jnp.where(lanes < BS, inner, first), second], axis=1)
        multiplier_ref[...] = jnp.where(wide >= BS, upper, 0.0)
        kept = jnp.where((full_col < BS) & (full_row < left + BS) & begun, 0.0, a)
        turn(a_ref, kept - stacked(multiplier, last), last)
        return carry

    lax.fori_loop(0, NB // BS, step_of, 0)
    turn(a_ref, a_ref[...], row_ref[...])
    linv_ref[...] = jnp.where(full_col <= full_row, a_ref[...], 0.0)
    band_ref[...] = -u_ref[...]
    upper_ref[...] = u_ref[...]


def reflector_factor(g_ref, linv_ref, refl_ref, a_ref, row_ref):
    rows, lanes, _ = block_iotas()
    full_row, full_col = ordering()
    top_block = exact(linv_ref[...], gathered_columns(g_ref, (2, 3)))
    unturned(top_block + (full_row == full_col).astype(F32), a_ref, row_ref)

    def step_of(step, carry):
        begun = step > 0
        a, last = a_ref[...], row_ref[...]
        kept = jnp.where((full_col < BS) & begun, 0.0, a)
        column = jnp.where(begun, a[:, :BS], 0.0)
        top = pltpu.roll(kept[BS : 2 * BS] - exact(column[BS : 2 * BS], last), NB - BS, 1)
        first, second = top[:, :LANES], top[:, LANES:]
        heads = lane_spread(first)
        first = jnp.where(lanes < BS, (rows == lanes).astype(F32), first)
        for j in range(BS):
            head = heads[j]
            inverse = 1.0 / head[j : j + 1]

            def put(value):
                scaled = value[j : j + 1] * inverse
                return jnp.where(rows == j, scaled, value - head * scaled)

            for k in range(j + 1, BS):
                heads[k] = put(heads[k])
            first, second = put(first), put(second)
        row_ref[...] = jnp.concatenate([first, second], axis=1)
        turn(a_ref, kept - exact(column, last), last)
        return carry

    lax.fori_loop(0, NB // BS, step_of, 0)
    a, last = a_ref[...], row_ref[...]
    turn(a_ref, jnp.where(full_col < BS, 0.0, a) - exact(a[:, :BS], last), last)
    refl_ref[...] = a_ref[...]


def reflector_kernel(g_ref, linv_ref, refl_ref, both_ref, a_ref, row_ref):
    reflector_factor(g_ref, linv_ref, refl_ref, a_ref, row_ref)
    both_ref[...] = product(split(refl_ref[...]), split(linv_ref[...]), 0, 0)


def tile_place(place, t, u):
    return t * N_ROW + place[0], u * N_COL + place[1]


def ordering():
    r = lax.broadcasted_iota(jnp.int32, (NB, NB), 0)
    c = lax.broadcasted_iota(jnp.int32, (NB, NB), 1)
    return r, c


def mirror_kernel(place, panel_ref, matrix_ref, keep_ref, send_ref, sum_ref):
    sum_ref[...] = jnp.zeros((NB, TC * NB), F32)
    for t in range(TR):
        rows = split(linear_tile(panel_ref, t))
        for u in range(TC):
            here = pl.ds(u * NB, NB)
            i, j = tile_place(place, t, u)

            @pl.when(i > j)
            def _():
                sum_ref[:, here] += product(rows, split(matrix_tile(matrix_ref, t, u)))

            @pl.when(i == j)
            def _():
                r, c = ordering()
                tile = jnp.where(r > c, matrix_tile(matrix_ref, t, u), 0.0)
                sum_ref[:, here] += product(rows, split(tile))

    for parity in range(2):

        @pl.when(place[0] % 2 == parity)
        def _():
            for k in range(N_ROW // 2):
                at = pl.ds(k * CHUNK, CHUNK)
                keep_ref[at, :] = sum_ref[pl.ds((2 * k + parity) * CHUNK, CHUNK), :]
                send_ref[at, :] = sum_ref[pl.ds((2 * k + 1 - parity) * CHUNK, CHUNK), :]


def row_copies(matrix_hbm, matrix_ref, sems, first):
    rows = matrix_ref.shape[0] // TR
    return [
        pltpu.make_async_copy(
            matrix_hbm.at[pl.ds(t * rows, rows)], matrix_ref.at[pl.ds(t * rows, rows)],
            sems.at[first + t],
        )
        for t in range(TR)
    ]


def symmetric_kernel(
    place, upper_ref, matrix_ref, panel_hbm, out_hbm, panel_ref, out_ref, sems
):
    panel_copy = pltpu.make_async_copy(panel_hbm, panel_ref, sems.at[0])
    panel_copy.start()
    out_copies = []
    factor = jnp.transpose(upper_ref[...])
    out_ref[...] = jnp.zeros((NB, TR * NB), F32)
    panel_copy.wait()
    cols = []
    for u in range(TC):
        value = gathered_tile(panel_ref, u)
        if u == 0:
            value = value + jnp.where(place[1] == 0, factor, 0.0)
        cols.append(split(value))
    for t in range(TR):
        here = pl.ds(t * NB, NB)
        for u in range(TC):
            i, j = tile_place(place, t, u)

            @pl.when(i > j)
            def _():
                out_ref[:, here] += product(cols[u], split(matrix_tile(matrix_ref, t, u)), 1, 1)

            @pl.when(i == j)
            def _():
                r, c = ordering()
                tile = jnp.where(r >= c, matrix_tile(matrix_ref, t, u), 0.0)
                out_ref[:, here] += product(cols[u], split(tile), 1, 1)

        if t == 0:

            @pl.when((place[0] == 0) & (place[1] == 0))
            def _():
                r, c = ordering()
                tile = jnp.where(r > c, matrix_tile(matrix_ref, 0, 0), 0.0)
                out_ref[:, here] += product(split(factor), split(tile))

        out_copies.append(
            pltpu.make_async_copy(out_ref.at[:, here], out_hbm.at[:, here], sems.at[1 + t])
        )
        out_copies[t].start()
    for copy in out_copies:
        copy.wait()


def vectors_kernel(
    place, linv_ref, panel_rows_ref, panel_cols_ref, rows_ref, cols_ref, vectors_ref,
):
    linv = split(linv_ref[...])
    r, c = ordering()
    eye = (r == c).astype(F32)
    for u in range(TC):
        value = product(linv, split(gathered_tile(panel_cols_ref, u)))
        if u == 0:
            value = value + jnp.where(place[1] == 0, eye, 0.0)
        cols_ref[:, pl.ds(u * NB, NB)] = value
    for t in range(TR):
        value = product(linv, split(linear_tile(panel_rows_ref, t)))
        if t == 0:
            value = value + jnp.where(place[0] == 0, eye, 0.0)
        rows_ref[:, pl.ds(t * NB, NB)] = value
    mine = rows_ref[pl.ds(pl.multiple_of(place[1] * SHARE, SHARE), SHARE), :]
    for piece in range(TR * 2):
        vectors_ref[pl.ds(piece, SHARE, TR * 2), :] = mine[:, piece * LANES : (piece + 1) * LANES]


PART = (TR + 1) * SHARE
DEAL = (TC + 1 + TR) * SHARE


def share_kernel(even_ref, odd_ref, recv_hbm, rows_hbm, out_ref, recv_ref, rows_ref, sems):
    recv_copy = pltpu.make_async_copy(recv_hbm, recv_ref, sems.at[0])
    rows_copy = pltpu.make_async_copy(rows_hbm, rows_ref, sems.at[1])
    recv_copy.start()
    rows_copy.start()
    recv_copy.wait()
    total = recv_ref[pl.ds(0, SHARE), :]
    for k in range(1, N_COL):
        total = total + recv_ref[pl.ds(k * SHARE, SHARE), :]
    mirrored = [even_ref[:, :NB], odd_ref[:, :NB], even_ref[:, NB:], odd_ref[:, NB:]]
    total = total + jnp.concatenate(mirrored, axis=1)
    for t in range(TR):
        out_ref[pl.ds(t * SHARE, SHARE), :] = total[:, t * NB : (t + 1) * NB]
    rows_copy.wait()
    out_ref[pl.ds(TR * SHARE, SHARE), :] = product(split(total), split(rows_ref[...]), 1, 1)


def deal_kernel(own_ref, part_ref, out_hbm, out_ref, sems):
    curved = part_ref[pl.ds(TR * SHARE, SHARE), :]
    for r in range(1, N_ROW):
        curved = curved + part_ref[pl.ds(r * PART + TR * SHARE, SHARE), :]
    own = own_ref[: TR * SHARE, :]
    copies = []
    group = N_COL // 4
    for c in range(N_COL):
        for u in range(TC):
            t = u * (N_COL // N_ROW) + c // N_ROW
            out_ref[pl.ds(c * DEAL + u * SHARE, SHARE), :] = part_ref[
                pl.ds((c % N_ROW) * PART + t * SHARE, SHARE), :
            ]
        out_ref[pl.ds(c * DEAL + TC * SHARE, SHARE), :] = curved
        out_ref[pl.ds(c * DEAL + (TC + 1) * SHARE, TR * SHARE), :] = own
        if c % group == group - 1:
            at = pl.ds((c + 1 - group) * DEAL, group * DEAL)
            copies.append(
                pltpu.make_async_copy(out_ref.at[at], out_hbm.at[at], sems.at[len(copies)])
            )
            copies[-1].start()
    for copy in copies:
        copy.wait()


def dealt(ref, slot):
    return jnp.concatenate(
        [ref[pl.ds(c * DEAL + slot * SHARE, SHARE), :] for c in range(N_COL)], axis=0
    )


def update_kernel(
    place, both_hbm, refl_hbm, dealt_hbm, cols_hbm, rows_hbm, matrix_hbm, out_hbm,
    both_ref, refl_ref, dealt_ref, cols_ref, rows_ref, matrix_ref, out_ref, sems,
):
    pairs = (
        (both_hbm, both_ref), (refl_hbm, refl_ref), (dealt_hbm, dealt_ref),
        (cols_hbm, cols_ref), (rows_hbm, rows_ref),
    )
    copies = [
        pltpu.make_async_copy(source, target, sems.at[k])
        for k, (source, target) in enumerate(pairs)
    ]
    matrix_copies = row_copies(matrix_hbm, matrix_ref, sems, len(copies))
    out_copies = row_copies(out_ref, out_hbm, sems, len(copies) + TR)
    for copy in copies + matrix_copies:
        copy.start()
    copies[0].wait()
    both = split(both_ref[...])
    copies[1].wait()
    refl = split(refl_ref[...])
    copies[2].wait()
    curved = split(product(both, split(dealt(dealt_ref, TC))))
    half_mixed = split(0.5 * product(curved, refl))
    copies[3].wait()
    sides = []
    for u in range(TC):
        vectors = cols_ref[:, pl.ds(u * NB, NB)]
        update = product(both, split(dealt(dealt_ref, u))) - product(half_mixed, split(vectors))
        sides.append(split(jnp.concatenate([update, vectors], axis=0)))
    copies[4].wait()
    for t in range(TR):
        here = pl.ds(t * NB, NB)
        vectors = rows_ref[:, here]
        update = product(both, split(dealt(dealt_ref, TC + 1 + t))) - product(
            half_mixed, split(vectors)
        )
        turned = split(jnp.concatenate([jnp.transpose(vectors), jnp.transpose(update)], axis=1))
        for u in range(TC):
            i, j = tile_place(place, t, u)
            if u == 0:
                matrix_copies[t].wait()

            @pl.when(i >= j)
            def _():
                value = matrix_tile(matrix_ref, t, u) - product(turned, sides[u])
                r, c = ordering()
                value = jnp.where((r >= c) | (i > j), value, 0.0)
                for half in range(2):
                    out_ref[matrix_rows(t, u, half), :] = value[:, half * LANES : (half + 1) * LANES]

            @pl.when(i < j)
            def _():
                for half in range(2):
                    out_ref[matrix_rows(t, u, half), :] = jnp.zeros((NB, LANES), F32)

        out_copies[t].start()
    for copy in out_copies:
        copy.wait()


def spread(value, axis, count):
    return lax.all_to_all(jnp.tile(value, (count, 1)), axis, 0, 0, tiled=True)


def routes():
    one, two = [], []
    for r in range(N_ROW):
        for c in range(N_COL):
            near = (c // 2) * N_COL + r
            far = near + N_ROW
            one.append((r * N_COL + c, far if c % 2 else near))
            two.append((r * N_COL + c, near if c % 2 else far))
    return one, two


def to_cols(even, odd, col_index):
    one, two = routes()
    flip, low = col_index % 2 == 1, col_index < N_ROW
    first = lax.ppermute(jnp.where(flip, odd, even), ("row", "col"), one)
    second = lax.ppermute(jnp.where(flip, even, odd), ("row", "col"), two)
    return jnp.where(low, first, second), jnp.where(low, second, first)


def to_rows(early, late, col_index):
    one, two = ([(there, here) for here, there in route] for route in routes())
    flip, low = col_index % 2 == 1, col_index < N_ROW
    first = lax.ppermute(jnp.where(low, early, late), ("row", "col"), one)
    second = lax.ppermute(jnp.where(low, late, early), ("row", "col"), two)
    return jnp.where(flip, second, first), jnp.where(flip, first, second)


def body(matrix, panel_t):
    row_index = lax.axis_index("row")
    col_index = lax.axis_index("col")
    place = jnp.stack([row_index, col_index]).astype(jnp.int32)
    stored = matrix.reshape(TR * NB * TC * 2, LANES)
    own = panel_t.reshape(SHARE * TR * 2, LANES)

    with jax.named_scope("panel"):
        by_tile = own.reshape(SHARE, TR, 2, LANES)
        chunk = to_cols(
            by_tile[:, 0::2].reshape(-1, LANES), by_tile[:, 1::2].reshape(-1, LANES), col_index
        )
        panel_rows, chunk = lax.optimization_barrier((spread(own, "col", N_COL), chunk))
    with jax.named_scope("gram"):
        (payload,) = call(
            gram_kernel, [(SPAN, LANES)], n_scalars=1, n_in=4, name="gram", moved=1 << 20
        )(place, own, *chunk, panel_rows)
        panel_cols = lax.all_gather(payload, "row", tiled=True)
        summed = panel_cols.reshape(N_ROW, SPAN, LANES)[:, CHUNK * TC * 2 :].sum(0)
        gram = spread(summed, "col", N_COL)
    with jax.named_scope("mirror"):
        keep, send = call(
            mirror_kernel, [(NB // 2, TC * NB)] * 2, scratch=[(NB, TC * NB)], n_scalars=1, n_in=2,
            name="mirror", moved=4 << 20,
        )(place, panel_rows, stored)
        mirror = keep + lax.ppermute(send, "row", [(r, r ^ 1) for r in range(N_ROW)])
        gram, mirror = lax.optimization_barrier((gram, mirror))
        parities = [list(range(parity, N_ROW, 2)) for parity in range(2)]
        mirror = lax.all_to_all(mirror, "row", 0, 0, axis_index_groups=parities, tiled=True)
        from_cols = mirror.reshape(N_ROW // 2, CHUNK, TC * NB).sum(0)
    with jax.named_scope("factor"):
        band, linv, upper = call(
            cholesky,
            [(NB, NB)] * 3,
            scratch=[(NB, NB)] * 2 + [(BS, NB)] * 2,
            n_in=1,
            name="cholesky",
            flops=5 * 10**9,
            moved=40 << 20,
        )(gram)
    with jax.named_scope("symmetric"):
        (row_terms,) = call(
            symmetric_kernel, [(NB, TR * NB)],
            scratch=[(N_ROW * SPAN, LANES), (NB, TR * NB)],
            n_scalars=1, n_in=2, n_any=1, any_out=True, copies=1 + TR,
            name="symmetric", moved=4 << 20,
        )(place, upper, stored, panel_cols)
    with jax.named_scope("vectors"):
        rows, cols, vectors = call(
            vectors_kernel,
            [(NB, TR * NB), (NB, TC * NB), (SHARE * TR * 2, LANES)],
            n_scalars=1,
            n_in=3,
            name="vectors",
            moved=4 << 20,
        )(place, linv, panel_rows, panel_cols)
    with jax.named_scope("sums"):
        received = lax.all_to_all(row_terms, "col", 0, 0, tiled=True)
        even, odd = to_rows(from_cols[:SHARE], from_cols[SHARE:], col_index)
        (payload,) = call(
            share_kernel, [(PART, NB)], scratch=[(NB, TR * NB)] * 2, n_in=2, n_any=2, copies=2,
            name="share", moved=2 << 20,
        )(even, odd, received, rows)
        parts = lax.all_gather(payload, "row", tiled=True)
    with jax.named_scope("deal"):
        (deal,) = call(
            deal_kernel, [(N_COL * DEAL, NB)], scratch=[(N_COL * DEAL, NB)], n_in=2, any_out=True,
            copies=4, name="deal", moved=3 << 20,
        )(payload, parts)
        deal, gram, linv = lax.optimization_barrier((deal, gram, linv))
        deal = lax.all_to_all(deal, "col", 0, 0, tiled=True)
    with jax.named_scope("reflector"):
        reflector, both = call(
            reflector_kernel,
            [(NB, NB)] * 2,
            scratch=[(NB, NB), (BS, NB)],
            n_in=2,
            name="reflector",
            flops=5 * 10**9,
            moved=40 << 20,
        )(gram, linv)
    with jax.named_scope("update"):
        (updated,) = call(
            update_kernel,
            [(TR * NB * TC * 2, LANES)],
            scratch=[
                (NB, NB),
                (NB, NB),
                (N_COL * DEAL, NB),
                (NB, TC * NB),
                (NB, TR * NB),
                (TR * NB * TC * 2, LANES),
                (TR * NB * TC * 2, LANES),
            ],
            n_scalars=1,
            n_in=0,
            n_any=6,
            any_out=True,
            copies=5 + 2 * TR,
            megabytes=60,
            name="update",
            moved=8 << 20,
        )(place, both, reflector, deal, cols, rows, stored)
    return (updated.reshape(matrix.shape), vectors.reshape(panel_t.shape), band, reflector)


def solution(mesh):
    placed = (P(None, "row", None, None, "col", None), P("col", None, "row", None))
    return jax.shard_map(
        body,
        mesh=mesh,
        in_specs=placed,
        out_specs=(P(None, "row", None, None, "col", None), P("col", None, "row", None), P(), P()),
        check_vma=False,
    )
```

```python
import jax
import jax.numpy as jnp
from jax import lax
from jax.experimental import pallas as pl
from jax.experimental.pallas import tpu as pltpu
from jax.sharding import PartitionSpec as P

NB = 256
TR = 4
TC = 2
N_ROW = 16
N_COL = 32
LANES = 128
BS = 16
SHARE = NB // N_COL
CHUNK = NB // N_ROW
F32 = jnp.float32
VMEM = pl.BlockSpec(memory_space=pltpu.VMEM)
SMEM = pl.BlockSpec(memory_space=pltpu.SMEM)


ANY = pl.BlockSpec(memory_space=pl.ANY)


def call(
    kernel, outs, scratch=(), n_scalars=0, n_in=1, n_any=0, any_out=False, copies=0,
    name=None, flops=0, moved=0, megabytes=40,
):
    buffers = [pltpu.VMEM(shape, F32) for shape in scratch]
    if copies:
        buffers.append(pltpu.SemaphoreType.DMA((copies,)))
    return pl.pallas_call(
        kernel,
        out_shape=[jax.ShapeDtypeStruct(shape, F32) for shape in outs],
        in_specs=[SMEM] * n_scalars + [VMEM] * n_in + [ANY] * n_any,
        out_specs=[ANY if any_out else VMEM] * len(outs),
        scratch_shapes=buffers,
        compiler_params=pltpu.CompilerParams(vmem_limit_bytes=megabytes * 2**20),
        cost_estimate=pl.CostEstimate(flops=flops, bytes_accessed=moved, transcendentals=0),
        name=name,
    )


def exact(a, b, ca=1, cb=0):
    return lax.dot_general(
        a,
        b,
        (((ca,), (cb,)), ((), ())),
        precision=lax.Precision.HIGHEST,
        preferred_element_type=F32,
    )


def split(a):
    high = a.astype(jnp.bfloat16)
    return high, (a - high.astype(F32)).astype(jnp.bfloat16)


def product(a, b, ca=1, cb=0):
    def one(x, y):
        return lax.dot_general(x, y, (((ca,), (cb,)), ((), ())), preferred_element_type=F32)

    return one(a[0], b[0]) + (one(a[0], b[1]) + one(a[1], b[0]))


def linear_tile(ref, t):
    return jnp.concatenate([ref[pl.ds(t * 2 + half, NB, TR * 2), :] for half in range(2)], axis=1)


SPAN = CHUNK * TC * 2 + 4 * SHARE


def gathered_tile(ref, u):
    return jnp.concatenate(
        [
            jnp.concatenate(
                [ref[pl.ds(k * SPAN + u * 2 + half, CHUNK, TC * 2), :] for k in range(N_ROW)], axis=0
            )
            for half in range(2)
        ],
        axis=1,
    )


def matrix_rows(t, u, half):
    return pl.ds((t * NB) * TC * 2 + u * 2 + half, NB, TC * 2)


def matrix_tile(ref, t, u):
    return jnp.concatenate([ref[matrix_rows(t, u, half), :] for half in range(2)], axis=1)


def gram_kernel(place, own_ref, early_ref, late_ref, panel_ref, out_ref):
    total = jnp.zeros((SHARE, NB), F32)
    for piece in range(TR * 2):
        total += exact(
            own_ref[pl.ds(piece, SHARE, TR * 2), :], panel_ref[pl.ds(piece, NB, TR * 2), :], 1, 1
        )
    half_chunk = SHARE * TC * 2
    out_ref[:half_chunk, :] = early_ref[...]
    out_ref[half_chunk : 2 * half_chunk, :] = late_ref[...]
    for half in range(2):
        at = 2 * half_chunk + half * SHARE
        out_ref[pl.ds(at, SHARE), :] = total[:, half * LANES : (half + 1) * LANES]
        top = own_ref[pl.ds(half, SHARE, TR * 2), :]
        out_ref[pl.ds(at + 2 * SHARE, SHARE), :] = jnp.where(place[0] == 0, top, 0.0)


def gathered_columns(g_ref, quarters):
    return jnp.concatenate(
        [
            jnp.concatenate(
                [g_ref[pl.ds((4 * k + q) * SHARE, SHARE), :] for k in range(N_COL)], axis=0
            )
            for q in quarters
        ],
        axis=1,
    )


def stacked(a, b):
    def three(x):
        high = x.astype(jnp.bfloat16)
        x = x - high.astype(F32)
        mid = x.astype(jnp.bfloat16)
        return high, mid, (x - mid.astype(F32)).astype(jnp.bfloat16)

    a1, a2, a3 = three(a)
    b1, b2, b3 = three(b)
    return lax.dot_general(
        jnp.concatenate([a1, a1, a1, a2, a2, a3], axis=0),
        jnp.concatenate([b1, b2, b3, b1, b2, b1], axis=0),
        (((0,), (0,)), ((), ())),
        preferred_element_type=F32,
    )


def block_iotas():
    rows = lax.broadcasted_iota(jnp.int32, (BS, LANES), 0)
    lanes = lax.broadcasted_iota(jnp.int32, (BS, LANES), 1)
    wide = lax.broadcasted_iota(jnp.int32, (BS, NB), 1)
    return rows, lanes, wide


def turn(a_ref, base, row):
    a_ref[: NB - BS, :] = pltpu.roll(base[BS:], NB - BS, 1)
    a_ref[NB - BS :, :] = pltpu.roll(row, NB - BS, 1)


def unturned(value, a_ref, row_ref):
    turned = pltpu.roll(value, BS, 1)
    a_ref[:BS, :] = turned[NB - BS :]
    a_ref[BS:, :] = turned[: NB - BS]
    row_ref[...] = turned[NB - BS :]


def lane_spread(first):
    return [jnp.broadcast_to(first[:, k : k + 1], (BS, LANES)) for k in range(BS)]


def cholesky(g_ref, band_ref, linv_ref, upper_ref, a_ref, u_ref, row_ref, multiplier_ref):
    rows, lanes, wide = block_iotas()
    full_row, full_col = ordering()
    unturned(gathered_columns(g_ref, (0, 1)), a_ref, row_ref)
    multiplier_ref[...] = jnp.zeros((BS, NB), F32)

    def step_of(step, carry):
        left = NB - BS * step
        begun = step > 0
        a, last, multiplier = a_ref[...], row_ref[...], multiplier_ref[...]
        top = jnp.where((wide < BS) & begun, 0.0, a[BS : 2 * BS])
        top = pltpu.roll(top - stacked(multiplier[:, BS : 2 * BS], last), NB - BS, 1)
        first, second = top[:, :LANES], top[:, LANES:]
        heads = lane_spread(first)
        inner = (rows == lanes).astype(F32)
        pivots = jnp.ones((BS, LANES), F32)
        for j in range(BS):
            pivot = heads[j][j : j + 1]
            factor = jnp.where(rows > j, heads[j], 0.0) * (1.0 / pivot)
            pivots = jnp.where(rows == j, pivot, pivots)
            for k in range(j + 1, BS):
                heads[k] = heads[k] - factor * heads[k][j : j + 1]
            first = first - factor * first[j : j + 1]
            second = second - factor * second[j : j + 1]
            inner = inner - factor * inner[j : j + 1]
        scale = lax.rsqrt(pivots)
        scale = scale * (1.5 - 0.5 * pivots * scale * scale)
        first, second, inner = first * scale, second * scale, inner * scale
        upper = jnp.concatenate([jnp.where(lanes >= rows, first, 0.0), second], axis=1)
        upper = jnp.where(wide < left, upper, 0.0)
        u_ref[pl.ds(pl.multiple_of(step * BS, BS), BS), :] = pltpu.roll(upper, step * BS, 1)
        row_ref[...] = jnp.concatenate([jnp.where(lanes < BS, inner, first), second], axis=1)
        multiplier_ref[...] = jnp.where(wide >= BS, upper, 0.0)
        kept = jnp.where((full_col < BS) & (full_row < left + BS) & begun, 0.0, a)
        turn(a_ref, kept - stacked(multiplier, last), last)
        return carry

    lax.fori_loop(0, NB // BS, step_of, 0)
    turn(a_ref, a_ref[...], row_ref[...])
    linv_ref[...] = jnp.where(full_col <= full_row, a_ref[...], 0.0)
    band_ref[...] = -u_ref[...]
    upper_ref[...] = u_ref[...]


def reflector_factor(g_ref, linv_ref, refl_ref, a_ref, row_ref):
    rows, lanes, _ = block_iotas()
    full_row, full_col = ordering()
    top_block = exact(linv_ref[...], gathered_columns(g_ref, (2, 3)))
    unturned(top_block + (full_row == full_col).astype(F32), a_ref, row_ref)

    def step_of(step, carry):
        begun = step > 0
        a, last = a_ref[...], row_ref[...]
        kept = jnp.where((full_col < BS) & begun, 0.0, a)
        column = jnp.where(begun, a[:, :BS], 0.0)
        top = pltpu.roll(kept[BS : 2 * BS] - exact(column[BS : 2 * BS], last), NB - BS, 1)
        first, second = top[:, :LANES], top[:, LANES:]
        heads = lane_spread(first)
        first = jnp.where(lanes < BS, (rows == lanes).astype(F32), first)
        for j in range(BS):
            head = heads[j]
            inverse = 1.0 / head[j : j + 1]

            def put(value):
                scaled = value[j : j + 1] * inverse
                return jnp.where(rows == j, scaled, value - head * scaled)

            for k in range(j + 1, BS):
                heads[k] = put(heads[k])
            first, second = put(first), put(second)
        row_ref[...] = jnp.concatenate([first, second], axis=1)
        turn(a_ref, kept - exact(column, last), last)
        return carry

    lax.fori_loop(0, NB // BS, step_of, 0)
    a, last = a_ref[...], row_ref[...]
    turn(a_ref, jnp.where(full_col < BS, 0.0, a) - exact(a[:, :BS], last), last)
    refl_ref[...] = a_ref[...]


def reflector_kernel(g_ref, linv_ref, refl_ref, both_ref, a_ref, row_ref):
    reflector_factor(g_ref, linv_ref, refl_ref, a_ref, row_ref)
    both_ref[...] = product(split(refl_ref[...]), split(linv_ref[...]), 0, 0)


def tile_place(place, t, u):
    return t * N_ROW + place[0], u * N_COL + place[1]


def ordering():
    r = lax.broadcasted_iota(jnp.int32, (NB, NB), 0)
    c = lax.broadcasted_iota(jnp.int32, (NB, NB), 1)
    return r, c


def mirror_kernel(place, panel_ref, matrix_ref, keep_ref, send_ref, sum_ref):
    sum_ref[...] = jnp.zeros((NB, TC * NB), F32)
    for t in range(TR):
        rows = split(linear_tile(panel_ref, t))
        for u in range(TC):
            here = pl.ds(u * NB, NB)
            i, j = tile_place(place, t, u)

            @pl.when(i > j)
            def _():
                sum_ref[:, here] += product(rows, split(matrix_tile(matrix_ref, t, u)))

            @pl.when(i == j)
            def _():
                r, c = ordering()
                tile = jnp.where(r > c, matrix_tile(matrix_ref, t, u), 0.0)
                sum_ref[:, here] += product(rows, split(tile))

    for parity in range(2):

        @pl.when(place[0] % 2 == parity)
        def _():
            for k in range(N_ROW // 2):
                at = pl.ds(k * CHUNK, CHUNK)
                keep_ref[at, :] = sum_ref[pl.ds((2 * k + parity) * CHUNK, CHUNK), :]
                send_ref[at, :] = sum_ref[pl.ds((2 * k + 1 - parity) * CHUNK, CHUNK), :]


def row_copies(matrix_hbm, matrix_ref, sems, first):
    rows = matrix_ref.shape[0] // TR
    return [
        pltpu.make_async_copy(
            matrix_hbm.at[pl.ds(t * rows, rows)], matrix_ref.at[pl.ds(t * rows, rows)],
            sems.at[first + t],
        )
        for t in range(TR)
    ]


def symmetric_kernel(
    place, upper_ref, matrix_ref, panel_hbm, out_hbm, panel_ref, out_ref, sems
):
    panel_copy = pltpu.make_async_copy(panel_hbm, panel_ref, sems.at[0])
    panel_copy.start()
    out_copies = []
    factor = jnp.transpose(upper_ref[...])
    out_ref[...] = jnp.zeros((NB, TR * NB), F32)
    panel_copy.wait()
    cols = []
    for u in range(TC):
        value = gathered_tile(panel_ref, u)
        if u == 0:
            value = value + jnp.where(place[1] == 0, factor, 0.0)
        cols.append(split(value))
    for t in range(TR):
        here = pl.ds(t * NB, NB)
        for u in range(TC):
            i, j = tile_place(place, t, u)

            @pl.when(i > j)
            def _():
                out_ref[:, here] += product(cols[u], split(matrix_tile(matrix_ref, t, u)), 1, 1)

            @pl.when(i == j)
            def _():
                r, c = ordering()
                tile = jnp.where(r >= c, matrix_tile(matrix_ref, t, u), 0.0)
                out_ref[:, here] += product(cols[u], split(tile), 1, 1)

        if t == 0:

            @pl.when((place[0] == 0) & (place[1] == 0))
            def _():
                r, c = ordering()
                tile = jnp.where(r > c, matrix_tile(matrix_ref, 0, 0), 0.0)
                out_ref[:, here] += product(split(factor), split(tile))

        out_copies.append(
            pltpu.make_async_copy(out_ref.at[:, here], out_hbm.at[:, here], sems.at[1 + t])
        )
        out_copies[t].start()
    for copy in out_copies:
        copy.wait()


def vectors_kernel(
    place, linv_ref, panel_rows_ref, panel_cols_ref, rows_ref, cols_ref, vectors_ref,
):
    linv = split(linv_ref[...])
    r, c = ordering()
    eye = (r == c).astype(F32)
    for u in range(TC):
        value = product(linv, split(gathered_tile(panel_cols_ref, u)))
        if u == 0:
            value = value + jnp.where(place[1] == 0, eye, 0.0)
        cols_ref[:, pl.ds(u * NB, NB)] = value
    for t in range(TR):
        value = product(linv, split(linear_tile(panel_rows_ref, t)))
        if t == 0:
            value = value + jnp.where(place[0] == 0, eye, 0.0)
        rows_ref[:, pl.ds(t * NB, NB)] = value
    mine = rows_ref[pl.ds(pl.multiple_of(place[1] * SHARE, SHARE), SHARE), :]
    for piece in range(TR * 2):
        vectors_ref[pl.ds(piece, SHARE, TR * 2), :] = mine[:, piece * LANES : (piece + 1) * LANES]


PART = (TR + 1) * SHARE
DEAL = (TC + 1 + TR) * SHARE


def share_kernel(even_ref, odd_ref, recv_hbm, rows_hbm, out_ref, recv_ref, rows_ref, sems):
    recv_copy = pltpu.make_async_copy(recv_hbm, recv_ref, sems.at[0])
    rows_copy = pltpu.make_async_copy(rows_hbm, rows_ref, sems.at[1])
    recv_copy.start()
    rows_copy.start()
    recv_copy.wait()
    total = recv_ref[pl.ds(0, SHARE), :]
    for k in range(1, N_COL):
        total = total + recv_ref[pl.ds(k * SHARE, SHARE), :]
    mirrored = [even_ref[:, :NB], odd_ref[:, :NB], even_ref[:, NB:], odd_ref[:, NB:]]
    total = total + jnp.concatenate(mirrored, axis=1)
    for t in range(TR):
        out_ref[pl.ds(t * SHARE, SHARE), :] = total[:, t * NB : (t + 1) * NB]
    rows_copy.wait()
    out_ref[pl.ds(TR * SHARE, SHARE), :] = product(split(total), split(rows_ref[...]), 1, 1)


def deal_kernel(own_ref, part_ref, out_hbm, out_ref, sems):
    curved = part_ref[pl.ds(TR * SHARE, SHARE), :]
    for r in range(1, N_ROW):
        curved = curved + part_ref[pl.ds(r * PART + TR * SHARE, SHARE), :]
    own = own_ref[: TR * SHARE, :]
    copies = []
    group = N_COL // 4
    for c in range(N_COL):
        for u in range(TC):
            t = u * (N_COL // N_ROW) + c // N_ROW
            out_ref[pl.ds(c * DEAL + u * SHARE, SHARE), :] = part_ref[
                pl.ds((c % N_ROW) * PART + t * SHARE, SHARE), :
            ]
        out_ref[pl.ds(c * DEAL + TC * SHARE, SHARE), :] = curved
        out_ref[pl.ds(c * DEAL + (TC + 1) * SHARE, TR * SHARE), :] = own
        if c % group == group - 1:
            at = pl.ds((c + 1 - group) * DEAL, group * DEAL)
            copies.append(
                pltpu.make_async_copy(out_ref.at[at], out_hbm.at[at], sems.at[len(copies)])
            )
            copies[-1].start()
    for copy in copies:
        copy.wait()


def dealt(ref, slot):
    return jnp.concatenate(
        [ref[pl.ds(c * DEAL + slot * SHARE, SHARE), :] for c in range(N_COL)], axis=0
    )


def update_kernel(
    place, both_hbm, refl_hbm, dealt_hbm, cols_hbm, rows_hbm, matrix_hbm, out_hbm,
    both_ref, refl_ref, dealt_ref, cols_ref, rows_ref, matrix_ref, out_ref, sems,
):
    pairs = (
        (both_hbm, both_ref), (refl_hbm, refl_ref), (dealt_hbm, dealt_ref),
        (cols_hbm, cols_ref), (rows_hbm, rows_ref),
    )
    copies = [
        pltpu.make_async_copy(source, target, sems.at[k])
        for k, (source, target) in enumerate(pairs)
    ]
    matrix_copies = row_copies(matrix_hbm, matrix_ref, sems, len(copies))
    out_copies = row_copies(out_ref, out_hbm, sems, len(copies) + TR)
    for copy in copies:
        copy.start()
    copies[0].wait()
    both = split(both_ref[...])
    copies[1].wait()
    refl = split(refl_ref[...])
    copies[2].wait()
    for copy in matrix_copies:
        copy.start()
    curved = split(product(both, split(dealt(dealt_ref, TC))))
    half_mixed = split(0.5 * product(curved, refl))
    copies[3].wait()
    sides = []
    for u in range(TC):
        vectors = cols_ref[:, pl.ds(u * NB, NB)]
        update = product(both, split(dealt(dealt_ref, u))) - product(half_mixed, split(vectors))
        sides.append(split(jnp.concatenate([update, vectors], axis=0)))
    copies[4].wait()
    for t in range(TR):
        here = pl.ds(t * NB, NB)
        vectors = rows_ref[:, here]
        update = product(both, split(dealt(dealt_ref, TC + 1 + t))) - product(
            half_mixed, split(vectors)
        )
        turned = split(jnp.concatenate([jnp.transpose(vectors), jnp.transpose(update)], axis=1))
        for u in range(TC):
            i, j = tile_place(place, t, u)
            if u == 0:
                matrix_copies[t].wait()

            @pl.when(i >= j)
            def _():
                value = matrix_tile(matrix_ref, t, u) - product(turned, sides[u])
                r, c = ordering()
                value = jnp.where((r >= c) | (i > j), value, 0.0)
                for half in range(2):
                    out_ref[matrix_rows(t, u, half), :] = value[:, half * LANES : (half + 1) * LANES]

            @pl.when(i < j)
            def _():
                for half in range(2):
                    out_ref[matrix_rows(t, u, half), :] = jnp.zeros((NB, LANES), F32)

        out_copies[t].start()
    for copy in out_copies:
        copy.wait()


def spread(value, axis, count):
    return lax.all_to_all(jnp.tile(value, (count, 1)), axis, 0, 0, tiled=True)


def routes():
    one, two = [], []
    for r in range(N_ROW):
        for c in range(N_COL):
            near = (c // 2) * N_COL + r
            far = near + N_ROW
            one.append((r * N_COL + c, far if c % 2 else near))
            two.append((r * N_COL + c, near if c % 2 else far))
    return one, two


def to_cols(even, odd, col_index):
    one, two = routes()
    flip, low = col_index % 2 == 1, col_index < N_ROW
    first = lax.ppermute(jnp.where(flip, odd, even), ("row", "col"), one)
    second = lax.ppermute(jnp.where(flip, even, odd), ("row", "col"), two)
    return jnp.where(low, first, second), jnp.where(low, second, first)


def to_rows(early, late, col_index):
    one, two = ([(there, here) for here, there in route] for route in routes())
    flip, low = col_index % 2 == 1, col_index < N_ROW
    first = lax.ppermute(jnp.where(low, early, late), ("row", "col"), one)
    second = lax.ppermute(jnp.where(low, late, early), ("row", "col"), two)
    return jnp.where(flip, second, first), jnp.where(flip, first, second)


def body(matrix, panel_t):
    row_index = lax.axis_index("row")
    col_index = lax.axis_index("col")
    place = jnp.stack([row_index, col_index]).astype(jnp.int32)
    stored = matrix.reshape(TR * NB * TC * 2, LANES)
    own = panel_t.reshape(SHARE * TR * 2, LANES)

    with jax.named_scope("panel"):
        by_tile = own.reshape(SHARE, TR, 2, LANES)
        chunk = to_cols(
            by_tile[:, 0::2].reshape(-1, LANES), by_tile[:, 1::2].reshape(-1, LANES), col_index
        )
        panel_rows, chunk = lax.optimization_barrier((spread(own, "col", N_COL), chunk))
    with jax.named_scope("gram"):
        (payload,) = call(
            gram_kernel, [(SPAN, LANES)], n_scalars=1, n_in=4, name="gram", moved=1 << 20
        )(place, own, *chunk, panel_rows)
        panel_cols = lax.all_gather(payload, "row", tiled=True)
        summed = panel_cols.reshape(N_ROW, SPAN, LANES)[:, CHUNK * TC * 2 :].sum(0)
        gram = spread(summed, "col", N_COL)
    with jax.named_scope("mirror"):
        keep, send = call(
            mirror_kernel, [(NB // 2, TC * NB)] * 2, scratch=[(NB, TC * NB)], n_scalars=1, n_in=2,
            name="mirror", moved=4 << 20,
        )(place, panel_rows, stored)
        mirror = keep + lax.ppermute(send, "row", [(r, r ^ 1) for r in range(N_ROW)])
        gram, mirror = lax.optimization_barrier((gram, mirror))
        parities = [list(range(parity, N_ROW, 2)) for parity in range(2)]
        mirror = lax.all_to_all(mirror, "row", 0, 0, axis_index_groups=parities, tiled=True)
        from_cols = mirror.reshape(N_ROW // 2, CHUNK, TC * NB).sum(0)
    with jax.named_scope("factor"):
        band, linv, upper = call(
            cholesky,
            [(NB, NB)] * 3,
            scratch=[(NB, NB)] * 2 + [(BS, NB)] * 2,
            n_in=1,
            name="cholesky",
            flops=5 * 10**9,
            moved=40 << 20,
        )(gram)
    with jax.named_scope("symmetric"):
        (row_terms,) = call(
            symmetric_kernel, [(NB, TR * NB)],
            scratch=[(N_ROW * SPAN, LANES), (NB, TR * NB)],
            n_scalars=1, n_in=2, n_any=1, any_out=True, copies=1 + TR,
            name="symmetric", moved=4 << 20,
        )(place, upper, stored, panel_cols)
    with jax.named_scope("vectors"):
        rows, cols, vectors = call(
            vectors_kernel,
            [(NB, TR * NB), (NB, TC * NB), (SHARE * TR * 2, LANES)],
            n_scalars=1,
            n_in=3,
            name="vectors",
            moved=4 << 20,
        )(place, linv, panel_rows, panel_cols)
    with jax.named_scope("sums"):
        received = lax.all_to_all(row_terms, "col", 0, 0, tiled=True)
        even, odd = to_rows(from_cols[:SHARE], from_cols[SHARE:], col_index)
        (payload,) = call(
            share_kernel, [(PART, NB)], scratch=[(NB, TR * NB)] * 2, n_in=2, n_any=2, copies=2,
            name="share", moved=2 << 20,
        )(even, odd, received, rows)
        parts = lax.all_gather(payload, "row", tiled=True)
    with jax.named_scope("deal"):
        (deal,) = call(
            deal_kernel, [(N_COL * DEAL, NB)], scratch=[(N_COL * DEAL, NB)], n_in=2, any_out=True,
            copies=4, name="deal", moved=3 << 20,
        )(payload, parts)
        deal, gram, linv = lax.optimization_barrier((deal, gram, linv))
        deal = lax.all_to_all(deal, "col", 0, 0, tiled=True)
    with jax.named_scope("reflector"):
        reflector, both = call(
            reflector_kernel,
            [(NB, NB)] * 2,
            scratch=[(NB, NB), (BS, NB)],
            n_in=2,
            name="reflector",
            flops=5 * 10**9,
            moved=40 << 20,
        )(gram, linv)
    with jax.named_scope("update"):
        (updated,) = call(
            update_kernel,
            [(TR * NB * TC * 2, LANES)],
            scratch=[
                (NB, NB),
                (NB, NB),
                (N_COL * DEAL, NB),
                (NB, TC * NB),
                (NB, TR * NB),
                (TR * NB * TC * 2, LANES),
                (TR * NB * TC * 2, LANES),
            ],
            n_scalars=1,
            n_in=0,
            n_any=6,
            any_out=True,
            copies=5 + 2 * TR,
            megabytes=60,
            name="update",
            moved=8 << 20,
        )(place, both, reflector, deal, cols, rows, stored)
    return (updated.reshape(matrix.shape), vectors.reshape(panel_t.shape), band, reflector)


def solution(mesh):
    placed = (P(None, "row", None, None, "col", None), P("col", None, "row", None))
    return jax.shard_map(
        body,
        mesh=mesh,
        in_specs=placed,
        out_specs=(P(None, "row", None, None, "col", None), P("col", None, "row", None), P(), P()),
        check_vma=False,
    )
```
